32 devices in a mesh: dp: 2 (over y), gz: 4 (over x, core), gy: 4 (over z).
Axes of the slice: x: 2, y: 2, z: 4, core: 2. Of those that a mesh axis runs over, the one named last changes fastest.
Arguments:
- volume: bfloat16 [2, 32, 32, 64, 256], P('dp', None, 'gz', 'gy'), may hold values from -6 to 6
- kernel_mid: bfloat16 [64, 32, 3, 3, 3], replicated, may hold values from -0.21875 to 0.21875
- kernel_deep: bfloat16 [128, 64, 3, 3, 3], replicated, may hold values from -0.15625 to 0.15625
- cotangent: bfloat16 [2, 128, 8, 16, 64], P('dp', None, 'gz', 'gy'), may hold values from -6 to 6
Outputs:
- mid_weight_grad: float32 [64, 32, 3, 3, 3], replicated
- deep_weight_grad: float32 [128, 64, 3, 3, 3], P('gy')
The draws below stay inside these ranges and needn't reach their ends.
All inputs are finite; a program needn't handle non-finite values.
Results may differ from the reference program's by a relative error of at most 0.0034.
Values may be sent and summed in bfloat16 or wider, within the bound.
No kernel may reach another device: no remote copies, remote signals or barrier semaphores. Data moves between devices by JAX's collectives and lax.ppermute only.
A program may use at most 128 MiB of HBM per device.

```python
import math
import jax
import jax.numpy as jnp
from jax import lax

C1 = 32
C2 = 64
C3 = 128
CX = 256
SAMPLES = 2
NZ = 32
NY = 64


def shard_levels(key, extent, split, low, top_value):
    gain, own = 1.0, jax.random.fold_in(key, 6)
    for axis_at, parts in split:
        steps = jnp.exp(jax.random.uniform(jax.random.fold_in(own, axis_at), (parts,), jnp.float32, low / len(split), top_value / len(split)))
        gain = gain * jnp.repeat(steps, extent[axis_at] // parts).reshape([-1 if axis == axis_at else 1 for axis in range(len(extent))])
    return gain


def scatter_about(rng, extent, scale, reach, shards=(), held_as=jnp.bfloat16):
    values = scale * jax.random.normal(rng, extent, jnp.float32)
    if shards:
        values = values * shard_levels(rng, extent, shards, -0.22, 0.18)
    return jnp.clip(values, -reach, reach).astype(held_as)


def setup_inputs(seed: int = 0) -> dict:
    streams_of = jax.random.split(jax.random.key(seed), 5)
    volume = scatter_about(streams_of[0], (SAMPLES, C1, NZ, NY, CX), 1.0, 6.0, ((0, 2), (2, 4), (3, 4)))
    kernel_mid = scatter_about(streams_of[1], (C2, C1, 3, 3, 3), (27 * C1) ** -0.5, 0.21875)
    kernel_deep = scatter_about(streams_of[2], (C3, C2, 3, 3, 3), (27 * C2) ** -0.5, 0.15625)
    cotangent = scatter_about(streams_of[3], (SAMPLES, C3, NZ // 4, NY // 4, CX // 4), 1.0, 6.0, ((0, 2), (2, 4), (3, 4)))
    return {"volume": volume, "kernel_mid": kernel_mid, "kernel_deep": kernel_deep, "cotangent": cotangent}


def conv_down(inputs, kernel, pads):
    return lax.conv_general_dilated(inputs, kernel, (2, 2, 2), pads, dimension_numbers=('NCDHW', 'OIDHW', 'NCDHW'), preferred_element_type=jnp.float32)

def kernel_grad(inputs, cot_field, pads):
    return lax.conv_general_dilated(inputs, cot_field, (1, 1, 1), pads, rhs_dilation=(2, 2, 2), dimension_numbers=('CNDHW', 'IODHW', 'CNDHW'), preferred_element_type=jnp.float32)

def input_grad(cot_field, kernel, pads):
    flipped = kernel[:, :, ::-1, ::-1, ::-1]
    return lax.conv_general_dilated(cot_field, flipped, (1, 1, 1), pads, lhs_dilation=(2, 2, 2), dimension_numbers=('NCDHW', 'IODHW', 'NCDHW'), preferred_element_type=jnp.float32)

def silu_slope(value):
    sigma = jax.nn.sigmoid(value)
    return sigma * (1.0 + value * (1.0 - sigma))

def reference(volume, kernel_mid, kernel_deep, cotangent):
    edge = ((1, 0), (1, 0), (1, 0))

    def one_sample(carry, items):
        sample = items[0][None]
        cot_field = items[1][None]
        pre_mid = conv_down(sample, kernel_mid, edge)
        active = jax.nn.silu(pre_mid).astype(jnp.bfloat16)
        deep_part = kernel_grad(active, cot_field, edge)
        back = input_grad(cot_field, kernel_deep, ((1, 2), (1, 2), (1, 2)))
        pre_grad = (back * silu_slope(pre_mid)).astype(jnp.bfloat16)
        mid_part = kernel_grad(sample, pre_grad, edge)
        return ((carry[0] + mid_part, carry[1] + deep_part), None)
    start = (jnp.zeros(kernel_mid.shape, jnp.float32), jnp.zeros(kernel_deep.shape, jnp.float32))
    (mid_sum, deep_sum), unused = lax.scan(one_sample, start, (volume, cotangent))
    count_mid = volume.shape[0] * (volume.shape[2] // 2) * (volume.shape[3] // 2) * (volume.shape[4] // 2)
    count_deep = cotangent.shape[0] * cotangent.shape[2] * cotangent.shape[3] * cotangent.shape[4]
    return (mid_sum / math.sqrt(count_mid), deep_sum / math.sqrt(count_deep))
```

```python
import functools
import math

import jax
import jax.numpy as jnp
from jax import lax
from jax.experimental import pallas as pl
from jax.experimental.pallas import tpu as pltpu
from jax.sharding import PartitionSpec as P

BF16 = jnp.bfloat16
F32 = jnp.float32
NN = (((1,), (0,)), ((), ()))
NT = (((1,), (1,)), ((), ()))


def dot(a, b, dims=NN):
    return lax.dot_general(a, b, dims, preferred_element_type=F32)


def passed_along(block, axis, distance):
    devices = range(lax.axis_size(axis))
    route = [(i - distance, i) for i in devices if i - distance in devices]
    return lax.ppermute(block, axis, route)


def picking_matrix(breadth):
    half = breadth // 2
    row = lax.broadcasted_iota(jnp.int32, (breadth, 3 * half), 0)
    col = lax.broadcasted_iota(jnp.int32, (breadth, 3 * half), 1)
    offset = (col >= half).astype(jnp.int32) + (col >= 2 * half).astype(jnp.int32)
    lane = col - offset * half
    odd = (lane >= half // 2).astype(jnp.int32)
    cell = 2 * (lane - odd * (half // 2)) + odd
    return jnp.where(row == 2 * cell + offset - 1, 1.0, 0.0).astype(BF16)


def put_rows(dst, start, value):
    dst[start : start + value.shape[0], :] = value


def main_kernel(dims, vol, below, beside, cot, cot_above, cot_beside, km, kd, out, even, odd, picked, pairs, act, back, slope, grad, sums):
    c1, c2, c3, depth, height, breadth, n_plane, n_gy = dims
    mz, my, mx = depth // 2, height // 2, breadth // 2
    dz, dy, dx = mz // 2, my // 2, mx // 2
    pick = picking_matrix(breadth)
    blk = 3 * c1

    def place(layer, row, piece):
        dst, at = (even, layer // 2) if layer % 2 == 0 else (odd, layer // 2)
        for a in range(3):
            dst[row * blk + a * c1 : row * blk + (a + 1) * c1, at * mx : (at + 1) * mx] = piece(a).astype(BF16)

    for layer in range(depth + 1):
        if layer == 0:
            rows = below[...]
        else:
            rows = vol[:, layer - 1].reshape(c1 * height, breadth)
        slot = layer % 2 * 3
        for a in range(3):
            picked[slot + a] = dot(rows, pick[:, a * mx : (a + 1) * mx])
        for y in range(height):
            place(layer, y + 1, lambda a: picked[slot + a, pl.ds(y, c1, stride=height), :])
        rim = dot(beside[layer], pick)
        place(layer, 0, lambda a: rim[:, a * mx : (a + 1) * mx])

    def windows(y):
        rows = slice(2 * y * blk, (2 * y + 3) * blk)
        return [even[rows, : mz * mx], odd[rows, :], even[rows, mx:]]

    for y in range(my):
        pre = dot(km[...], jnp.concatenate(windows(y), axis=0))
        sigma = jax.nn.sigmoid(pre)
        slope[y] = sigma * (1.0 + pre * (1.0 - sigma))
        active = (pre * sigma).astype(BF16)
        for z in range(mz):
            cls = (z % 2) * 2 + y % 2
            at = (z // 2) * dy + y // 2
            act[cls * c2 : (cls + 1) * c2, at * mx : (at + 1) * mx] = active[:, z * mx : (z + 1) * mx]

    zero = jnp.zeros((dx, c3), BF16)
    last = lax.broadcasted_iota(jnp.int32, (dx, c3), 0) == dx - 1
    for z in range(dz + 1):
        for y in range(dy + 1):
            if y == dy:
                here = cot_beside[z]
            elif z == dz:
                here = cot_above[y]
            else:
                here = cot[z, y]
            moved = jnp.where(last, 0.0, pltpu.roll(here.astype(F32), dx - 1, 0)).astype(BF16)
            top = (z * (dy + 1) + y) * mx
            pairs[top : top + dx, :] = jnp.concatenate([zero, here, zero], axis=1)
            pairs[top + dx : top + mx, :] = jnp.concatenate([moved, zero, here], axis=1)

    def shifted(sz, sy, z):
        top = ((z + sz) * (dy + 1) + sy) * mx
        return pairs[top : top + dy * mx, :]

    deep = {}
    span = dy * mx
    for sz in range(2):
        for sy in range(2):
            classes = [(pz, py) for pz in range(2) for py in range(2) if pz >= sz and py >= sy]
            taps = [(0 if sz else 1 + pz, 0 if sy else 1 + py) for pz, py in classes]
            lhs = jnp.concatenate([act[(pz * 2 + py) * c2 : (pz * 2 + py + 1) * c2, :] for pz, py in classes], axis=0)
            filters = jnp.concatenate(
                [jnp.concatenate([kd[(az * 3 + ay) * 3 + ax] for ax in range(3)], axis=1) for az, ay in taps], axis=0
            )
            total = None
            for z in range(dz):
                term = dot(lhs[:, z * span : (z + 1) * span], shifted(sz, sy, z))
                total = term if total is None else total + term
                grads = dot(filters, shifted(sz, sy, z), NT)
                for n, (pz, py) in enumerate(classes):
                    rows = slice((pz * 2 + py) * c2, (pz * 2 + py + 1) * c2)
                    piece = grads[n * c2 : (n + 1) * c2]
                    if sz or sy:
                        piece = piece + back[rows, z * span : (z + 1) * span]
                    back[rows, z * span : (z + 1) * span] = piece
            for n, (az, ay) in enumerate(taps):
                for ax in range(3):
                    deep[(az * 3 + ay) * 3 + ax] = total[n * c2 : (n + 1) * c2, ax * c3 : (ax + 1) * c3]

    for y in range(my):
        for z in range(mz):
            cls = (z % 2) * 2 + y % 2
            at = (z // 2) * dy + y // 2
            value = back[cls * c2 : (cls + 1) * c2, at * mx : (at + 1) * mx] * slope[y, :, z * mx : (z + 1) * mx]
            grad[y, :, z * mx : (z + 1) * mx] = value.astype(BF16)

    mids = []
    for az in range(3):
        total = None
        for y in range(my):
            term = dot(windows(y)[az], grad[y], NT)
            total = term if total is None else total + term
        mids.append(total)
    mid = jnp.concatenate(mids, axis=0)

    share = c3 // n_gy
    slabs = 14
    deep_rows = slabs * share // n_plane
    mid_rows = 448 // n_plane
    chunk = deep_rows + mid_rows

    def spread(value, first, per, gys, offset):
        done = 0
        while done < value.shape[0]:
            k, r = divmod(first + done, per)
            count = min(per - r, value.shape[0] - done)
            for g in gys:
                put_rows(sums, (k * n_gy + g) * chunk + offset + r, value[done : done + count])
            done += count

    for slab in range(slabs):
        second = deep[2 * slab + 1] if 2 * slab + 1 < 27 else jnp.zeros((c2, c3), F32)
        turned = jnp.concatenate([deep[2 * slab], second], axis=0).T
        for g in range(n_gy):
            spread(turned[g * share : (g + 1) * share], slab * share, deep_rows, [g], 0)
    half = mid.shape[0] // 2
    packed = jnp.concatenate([mid[:half], mid[half:]], axis=1)
    packed = jnp.concatenate([packed, jnp.zeros((448 - half, 128), F32)], axis=0)
    spread(packed, 0, mid_rows, range(n_gy), deep_rows)
    out[...] = sums[...].astype(BF16)


def last_kernel(dims, scales, got, mid_out, deep_out):
    n_plane, share, c2, deep_rows, mid_rows = dims
    whole = got[...]
    deep = whole[:, :deep_rows].reshape(n_plane * deep_rows, 128) * scales[1]
    mid = whole[:, deep_rows:].reshape(n_plane * mid_rows, 128) * scales[0]
    for a in range(27):
        deep_out[a] = deep[(a // 2) * share : (a // 2 + 1) * share, (a % 2) * c2 : (a % 2 + 1) * c2]
    mid_out[:432] = mid[:432, :64]
    mid_out[432:] = mid[:432, 64:]


def on_device(volume, kernel_mid, kernel_deep, cotangent):
    n_dp = lax.axis_size("dp")
    n_gz = lax.axis_size("gz")
    n_gy = lax.axis_size("gy")
    samples, c1, depth, height, breadth = volume.shape
    c2, c3 = kernel_mid.shape[0], kernel_deep.shape[0]
    count_mid = n_dp * samples * (n_gz * depth // 2) * (n_gy * height // 2) * (breadth // 2)
    count_deep = n_dp * samples * (n_gz * depth // 4) * (n_gy * height // 4) * (breadth // 4)
    mz, my, mx = depth // 2, height // 2, breadth // 2
    dz, dy, dx = mz // 2, my // 2, mx // 2
    n_plane = n_dp * n_gz
    vol = volume[0]
    cot = cotangent[0].transpose(1, 2, 3, 0)
    below = passed_along(vol[:, -1], "gz", 1)
    cot_above = passed_along(cot[0], "gz", -1)
    edge = jnp.concatenate([below[None, :, -1], vol[:, :, -1].transpose(1, 0, 2)], axis=0)
    beside = passed_along(edge, "gy", 1)
    cot_edge = jnp.concatenate([cot[:, 0], cot_above[None, 0]], axis=0)
    cot_beside = passed_along(cot_edge, "gy", -1)
    km = kernel_mid.transpose(2, 3, 4, 1, 0).reshape(27 * c1, c2).T
    kd = kernel_deep.transpose(2, 3, 4, 1, 0).reshape(27, c2, c3)

    share = c3 // n_gy
    deep_rows = 14 * share // n_plane
    mid_rows = 448 // n_plane
    chunk = deep_rows + mid_rows
    total_rows = n_plane * n_gy * chunk
    rows = 3 * c1 * (height + 1)
    sent = pl.pallas_call(
        functools.partial(main_kernel, (c1, c2, c3, depth, height, breadth, n_plane, n_gy)),
        out_shape=jax.ShapeDtypeStruct((total_rows, 128), BF16),
        in_specs=[pl.BlockSpec(memory_space=pltpu.VMEM)] * 8,
        out_specs=pl.BlockSpec(memory_space=pltpu.VMEM),
        scratch_shapes=[
            pltpu.VMEM((rows, (mz + 1) * mx), BF16),
            pltpu.VMEM((rows, mz * mx), BF16),
            pltpu.VMEM((6, c1 * height, mx), F32),
            pltpu.VMEM(((dz + 1) * (dy + 1) * mx, 3 * c3), BF16),
            pltpu.VMEM((4 * c2, dz * dy * mx), BF16),
            pltpu.VMEM((4 * c2, dz * dy * mx), F32),
            pltpu.VMEM((my, c2, mz * mx), F32),
            pltpu.VMEM((my, c2, mz * mx), BF16),
            pltpu.VMEM((total_rows, 128), F32),
        ],
        compiler_params=pltpu.CompilerParams(vmem_limit_bytes=48 * 1024 * 1024),
    )(vol, below.reshape(c1 * height, breadth), beside, cot, cot_above, cot_beside, km, kd)
    got = lax.all_to_all(sent.reshape(n_plane * n_gy, chunk, 128), ("dp", "gz", "gy"), 0, 0)
    own = jnp.sum(got.astype(F32), axis=0)
    whole = lax.all_gather(own, ("dp", "gz"), axis=0)
    scales = (1.0 / math.sqrt(count_mid), 1.0 / math.sqrt(count_deep))
    mid, deep = pl.pallas_call(
        functools.partial(last_kernel, (n_plane, share, c2, deep_rows, mid_rows), scales),
        out_shape=(jax.ShapeDtypeStruct((27 * c1, c2), F32), jax.ShapeDtypeStruct((27, share, c2), F32)),
        in_specs=[pl.BlockSpec(memory_space=pltpu.VMEM)],
        out_specs=(pl.BlockSpec(memory_space=pltpu.VMEM), pl.BlockSpec(memory_space=pltpu.VMEM)),
        compiler_params=pltpu.CompilerParams(vmem_limit_bytes=24 * 1024 * 1024),
    )(whole)
    mid = mid.reshape(3, 3, 3, c1, c2).transpose(4, 3, 0, 1, 2)
    deep = deep.reshape(3, 3, 3, share, c2).transpose(3, 4, 0, 1, 2)
    return mid, deep


def solution(mesh):
    in_specs = (P("dp", None, "gz", "gy", None), P(), P(), P("dp", None, "gz", "gy", None))
    out_specs = (P(), P("gy", None, None, None, None))
    return jax.shard_map(
        on_device, mesh=mesh, in_specs=in_specs, out_specs=out_specs, check_vma=False
    )
```

```python
import functools
import math

import jax
import jax.numpy as jnp
from jax import lax
from jax.experimental import pallas as pl
from jax.experimental.pallas import tpu as pltpu
from jax.sharding import Mesh, PartitionSpec as P

BF16 = jnp.bfloat16
F32 = jnp.float32
NN = (((1,), (0,)), ((), ()))
NT = (((1,), (1,)), ((), ()))


def dot(a, b, dims=NN):
    return lax.dot_general(a, b, dims, preferred_element_type=F32)


def passed_along(block, axis, distance):
    devices = range(lax.axis_size(axis))
    route = [(i - distance, i) for i in devices if i - distance in devices]
    return lax.ppermute(block, axis, route)


def picking_matrix(breadth):
    half = breadth // 2
    row = lax.broadcasted_iota(jnp.int32, (breadth, 3 * half), 0)
    col = lax.broadcasted_iota(jnp.int32, (breadth, 3 * half), 1)
    offset = (col >= half).astype(jnp.int32) + (col >= 2 * half).astype(jnp.int32)
    lane = col - offset * half
    odd = (lane >= half // 2).astype(jnp.int32)
    cell = 2 * (lane - odd * (half // 2)) + odd
    return jnp.where(row == 2 * cell + offset - 1, 1.0, 0.0).astype(BF16)


def place(dst, row, lanes, piece):
    c1 = piece(0).shape[0]
    for a in range(3):
        dst[row + a * c1 : row + (a + 1) * c1, lanes] = piece(a).astype(BF16)


def spread_layer(rows, pick, picked, c1, height, mx, put):
    for a in range(3):
        picked[a] = dot(rows, pick[:, a * mx : (a + 1) * mx])
    for y in range(height):
        put(y, lambda a: picked[a, pl.ds(y, c1, stride=height), :])


def edge_kernel(dims, vol, layer, side, tall):
    c1, depth, height, breadth = dims
    layer[...] = vol[:, depth - 1].reshape(c1 * height, breadth)
    side[0] = jnp.zeros((c1, breadth), BF16)
    for z in range(depth):
        top = vol[:, z].astype(F32)[:, height - 8 :].reshape(c1 * 8, breadth)
        for part in range(breadth // 128):
            lanes = slice(part * 128, (part + 1) * 128)
            slot = (z * (breadth // 128) + part) % 4
            tall[slot] = top[:, lanes]
            side[z + 1, :, lanes] = tall[slot, pl.ds(7, c1, stride=8), :].astype(BF16)


def gather_kernel(dims, vol, even, odd, picked):
    c1, depth, height, breadth = dims
    mx = breadth // 2
    pick = picking_matrix(breadth)
    for layer in range(depth):
        rows = vol[:, layer].reshape(c1 * height, breadth)
        dst = even if layer % 2 else odd
        lanes = slice(layer // 2 * mx, (layer // 2 + 1) * mx)
        put = lambda y, piece: place(dst, y * 3 * c1, lanes, piece)
        spread_layer(rows, pick, picked.at[layer % 2], c1, height, mx, put)


def main_kernel(dims, even, odd, below, beside, cot, cot_above, cot_beside, km, kd, me, keep, send, rim_z, rim_even, rim_odd, picked, pairs, act, back, slope, grad, sums):
    c1, c2, c3, depth, height, breadth, n_pl, n_gy = dims
    mz, my, mx = depth // 2, height // 2, breadth // 2
    dz, dy, dx = mz // 2, my // 2, mx // 2
    pick = picking_matrix(breadth)
    blk = 3 * c1

    put = lambda y, piece: place(rim_z, (y + 1) * blk, slice(0, mx), piece)
    spread_layer(below[...], pick, picked, c1, height, mx, put)
    for layer in range(depth + 1):
        rim = dot(beside[layer], pick)
        if layer == 0:
            dst, at = rim_z, 0
        else:
            dst, at = (rim_odd, layer // 2) if layer % 2 else (rim_even, layer // 2 - 1)
        place(dst, 0, slice(at * mx, (at + 1) * mx), lambda a: rim[:, a * mx : (a + 1) * mx])

    def window(y, az):
        source, rim = (odd, rim_odd) if az == 1 else (even, rim_even)
        if y == 0:
            cells = jnp.concatenate([rim[...], source[: 2 * blk, :]], axis=0)
        else:
            cells = source[(2 * y - 1) * blk : (2 * y + 2) * blk, :]
        if az == 0:
            cells = jnp.concatenate([rim_z[2 * y * blk : (2 * y + 3) * blk, :], cells[:, : (mz - 1) * mx]], axis=1)
        return cells

    turned_km = km[...].astype(F32).T.astype(BF16)
    for y in range(my):
        pre = dot(turned_km, jnp.concatenate([window(y, az) for az in range(3)], axis=0))
        sigma = jax.nn.sigmoid(pre)
        slope[y] = sigma * (1.0 + pre * (1.0 - sigma))
        active = (pre * sigma).astype(BF16)
        for z in range(mz):
            cls = (z % 2) * 2 + y % 2
            at = (z // 2) * dy + y // 2
            act[cls * c2 : (cls + 1) * c2, at * mx : (at + 1) * mx] = active[:, z * mx : (z + 1) * mx]

    zero = jnp.zeros((dx, c3), BF16)
    last = lax.broadcasted_iota(jnp.int32, (dx, c3), 0) == dx - 1
    for z in range(dz + 1):
        for y in range(dy + 1):
            if y == dy:
                here = cot_beside[z]
            elif z == dz:
                here = cot_above[y]
            else:
                here = cot[z, y]
            moved = jnp.where(last, 0.0, pltpu.roll(here.astype(F32), dx - 1, 0)).astype(BF16)
            top = (z * (dy + 1) + y) * mx
            pairs[top : top + dx, :] = jnp.concatenate([zero, here, zero], axis=1)
            pairs[top + dx : top + mx, :] = jnp.concatenate([moved, zero, here], axis=1)

    def shifted(sz, sy, z):
        top = ((z + sz) * (dy + 1) + sy) * mx
        return pairs[top : top + dy * mx, :]

    deep = {}
    span = dy * mx
    for sz in range(2):
        for sy in range(2):
            classes = [(pz, py) for pz in range(2) for py in range(2) if pz >= sz and py >= sy]
            taps = [(0 if sz else 1 + pz, 0 if sy else 1 + py) for pz, py in classes]
            lhs = jnp.concatenate([act[(pz * 2 + py) * c2 : (pz * 2 + py + 1) * c2, :] for pz, py in classes], axis=0)
            filters = jnp.concatenate(
                [jnp.concatenate([kd[(az * 3 + ay) * 3 + ax] for ax in range(3)], axis=1) for az, ay in taps], axis=0
            )
            total = None
            for z in range(dz):
                term = dot(lhs[:, z * span : (z + 1) * span], shifted(sz, sy, z))
                total = term if total is None else total + term
                grads = dot(filters, shifted(sz, sy, z), NT)
                for n, (pz, py) in enumerate(classes):
                    rows = slice((pz * 2 + py) * c2, (pz * 2 + py + 1) * c2)
                    piece = grads[n * c2 : (n + 1) * c2]
                    if sz or sy:
                        piece = piece + back[rows, z * span : (z + 1) * span]
                    back[rows, z * span : (z + 1) * span] = piece
            for n, (az, ay) in enumerate(taps):
                for ax in range(3):
                    deep[(az * 3 + ay) * 3 + ax] = total[n * c2 : (n + 1) * c2, ax * c3 : (ax + 1) * c3]

    for y in range(my):
        for z in range(mz):
            cls = (z % 2) * 2 + y % 2
            at = (z // 2) * dy + y // 2
            value = back[cls * c2 : (cls + 1) * c2, at * mx : (at + 1) * mx] * slope[y, :, z * mx : (z + 1) * mx]
            grad[y, :, z * mx : (z + 1) * mx] = value.astype(BF16)

    mids = []
    for az in range(3):
        total = None
        for y in range(my):
            term = dot(window(y, az), grad[y], NT)
            total = term if total is None else total + term
        mids.append(total)
    mid = jnp.concatenate(mids, axis=0)

    share = c3 // n_gy
    per = 448 // (2 * n_pl)
    chunk = (n_gy + 1) * per

    def spread(value, first, offset):
        done = 0
        while done < value.shape[0]:
            k, r = divmod(first + done, per)
            count = min(per - r, value.shape[0] - done)
            core, start = k % 2, k // 2 * chunk + offset + r
            sums[core, start : start + count, :] = value[done : done + count]
            done += count

    for slab in range(14):
        second = deep[2 * slab + 1] if 2 * slab + 1 < 27 else jnp.zeros((c2, c3), F32)
        turned = jnp.concatenate([deep[2 * slab], second], axis=0).T
        for g in range(n_gy):
            spread(turned[g * share : (g + 1) * share], slab * share, g * per)
    half = mid.shape[0] // 2
    packed = jnp.concatenate([mid[:half], mid[half:]], axis=1)
    packed = jnp.concatenate([packed, jnp.zeros((448 - half, 128), F32)], axis=0)
    spread(packed, 0, n_gy * per)
    keep[...] = sums[me[0]]
    send[...] = sums[1 - me[0]]


def last_kernel(dims, scales, got, mid_out, deep_out):
    n_all, share, c2, per = dims
    whole = got[...]
    deep = whole[:, :per].reshape(n_all * per, 128) * scales[1]
    mid = whole[:, per:].reshape(n_all * per, 128) * scales[0]
    for a in range(27):
        deep_out[a] = deep[(a // 2) * share : (a // 2 + 1) * share, (a % 2) * c2 : (a % 2 + 1) * c2]
    mid_out[:432] = mid[:432, :64]
    mid_out[432:] = mid[:432, 64:]


def on_device(volume, kernel_mid, kernel_deep, cotangent):
    n_dp = lax.axis_size("dp")
    gz = ("gx", "core")
    n_gz = lax.axis_size(gz)
    n_gy = lax.axis_size("gy")
    samples, c1, depth, height, breadth = volume.shape
    c2, c3 = kernel_mid.shape[0], kernel_deep.shape[0]
    count_mid = n_dp * samples * (n_gz * depth // 2) * (n_gy * height // 2) * (breadth // 2)
    count_deep = n_dp * samples * (n_gz * depth // 4) * (n_gy * height // 4) * (breadth // 4)
    mz, my, mx = depth // 2, height // 2, breadth // 2
    dz, dy, dx = mz // 2, my // 2, mx // 2
    n_pl = n_dp * n_gz // 2
    vol = volume[0]
    cot = cotangent[0].transpose(1, 2, 3, 0)
    in_vmem = pl.BlockSpec(memory_space=pltpu.VMEM)
    layer, side = pl.pallas_call(
        functools.partial(edge_kernel, (c1, depth, height, breadth)),
        out_shape=(
            jax.ShapeDtypeStruct((c1 * height, breadth), BF16),
            jax.ShapeDtypeStruct((depth + 1, c1, breadth), BF16),
        ),
        in_specs=[in_vmem],
        out_specs=(in_vmem, in_vmem),
        scratch_shapes=[pltpu.VMEM((4, c1 * 8, 128), F32)],
        compiler_params=pltpu.CompilerParams(vmem_limit_bytes=16 * 1024 * 1024),
    )(vol)
    below = passed_along(layer, gz, 1)
    cot_above = passed_along(cot[0], gz, -1)
    edge = side.at[0].set(below.reshape(c1, height, breadth)[:, -1])
    beside = passed_along(edge, "gy", 1)
    cot_edge = jnp.concatenate([cot[:, 0], cot_above[None, 0]], axis=0)
    cot_beside = passed_along(cot_edge, "gy", -1)
    km = kernel_mid.transpose(2, 3, 4, 1, 0).reshape(27 * c1, c2)
    kd = kernel_deep.transpose(2, 3, 4, 1, 0).reshape(27, c2, c3)

    share = c3 // n_gy
    per = 448 // (2 * n_pl)
    chunk = (n_gy + 1) * per
    me = lax.axis_index("core").reshape(1)
    blk = 3 * c1
    own_cells = jax.ShapeDtypeStruct((height * blk, mz * mx), BF16)
    even, odd = pl.pallas_call(
        functools.partial(gather_kernel, (c1, depth, height, breadth)),
        out_shape=(own_cells, own_cells),
        in_specs=[in_vmem],
        out_specs=(in_vmem, in_vmem),
        scratch_shapes=[pltpu.VMEM((2, 3, c1 * height, mx), F32)],
        cost_estimate=pl.CostEstimate(flops=2 * c1 * depth * height * breadth * 3 * mx, bytes_accessed=8 << 20, transcendentals=0),
        compiler_params=pltpu.CompilerParams(vmem_limit_bytes=24 * 1024 * 1024),
    )(vol)
    keep, send = pl.pallas_call(
        functools.partial(main_kernel, (c1, c2, c3, depth, height, breadth, n_pl, n_gy)),
        out_shape=(jax.ShapeDtypeStruct((n_pl * chunk, 128), F32), jax.ShapeDtypeStruct((n_pl * chunk, 128), F32)),
        in_specs=[in_vmem] * 9 + [pl.BlockSpec(memory_space=pltpu.SMEM)],
        out_specs=(in_vmem, in_vmem),
        scratch_shapes=[
            pltpu.VMEM(((height + 1) * blk, mx), BF16),
            pltpu.VMEM((blk, mz * mx), BF16),
            pltpu.VMEM((blk, mz * mx), BF16),
            pltpu.VMEM((3, c1 * height, mx), F32),
            pltpu.VMEM(((dz + 1) * (dy + 1) * mx, 3 * c3), BF16),
            pltpu.VMEM((4 * c2, dz * dy * mx), BF16),
            pltpu.VMEM((4 * c2, dz * dy * mx), F32),
            pltpu.VMEM((my, c2, mz * mx), F32),
            pltpu.VMEM((my, c2, mz * mx), BF16),
            pltpu.VMEM((2, n_pl * chunk, 128), F32),
        ],
        compiler_params=pltpu.CompilerParams(vmem_limit_bytes=48 * 1024 * 1024),
    )(even, odd, below, beside, cot, cot_above, cot_beside, km, kd, me)
    other = lax.ppermute(send, "core", [(0, 1), (1, 0)])
    pair = (keep + other).astype(BF16).reshape(n_pl, chunk, 128)
    own = jnp.sum(lax.all_to_all(pair, ("dp", "gx"), 0, 0).astype(F32), axis=0)
    deep_own = own[: n_gy * per].reshape(n_gy, per, 128)
    mid_own = jnp.broadcast_to(own[n_gy * per :], (n_gy, per, 128))
    column = jnp.concatenate([deep_own, mid_own], axis=1).astype(BF16)
    own = jnp.sum(lax.all_to_all(column, "gy", 0, 0).astype(F32), axis=0)
    whole = lax.all_gather(own, ("dp", "gx", "core"), axis=0)
    scales = (1.0 / math.sqrt(count_mid), 1.0 / math.sqrt(count_deep))
    mid, deep = pl.pallas_call(
        functools.partial(last_kernel, (2 * n_pl, share, c2, per), scales),
        out_shape=(jax.ShapeDtypeStruct((27 * c1, c2), F32), jax.ShapeDtypeStruct((27, share, c2), F32)),
        in_specs=[in_vmem],
        out_specs=(in_vmem, in_vmem),
        compiler_params=pltpu.CompilerParams(vmem_limit_bytes=24 * 1024 * 1024),
    )(whole)
    mid = mid.reshape(3, 3, 3, c1, c2).transpose(4, 3, 0, 1, 2)
    deep = deep.reshape(3, 3, 3, share, c2).transpose(3, 4, 0, 1, 2)
    return mid, deep


def solution(mesh):
    n_dp, n_gz, n_gy = (mesh.shape[name] for name in ("dp", "gz", "gy"))
    split = Mesh(mesh.devices.reshape(n_dp, n_gz // 2, 2, n_gy), ("dp", "gx", "core", "gy"))
    by_cells = P("dp", None, ("gx", "core"), "gy", None)
    in_specs = (by_cells, P(), P(), by_cells)
    out_specs = (P(), P("gy", None, None, None, None))
    return jax.shard_map(
        on_device, mesh=split, in_specs=in_specs, out_specs=out_specs, check_vma=False
    )
```

```python
import functools
import math

import jax
import jax.numpy as jnp
from jax import lax
from jax.experimental import pallas as pl
from jax.experimental.pallas import tpu as pltpu
from jax.sharding import Mesh, PartitionSpec as P

BF16 = jnp.bfloat16
F32 = jnp.float32
NN = (((1,), (0,)), ((), ()))
NT = (((1,), (1,)), ((), ()))


def dot(a, b, dims=NN):
    return lax.dot_general(a, b, dims, preferred_element_type=F32)


def swapped(block, axis, first):
    count = lax.axis_size(axis)
    route = [(i, i + 1) for i in range(first, count - 1, 2)]
    return lax.ppermute(block, axis, route + [(j, i) for i, j in route])


def picking_matrix(breadth):
    half = breadth // 2
    row = lax.broadcasted_iota(jnp.int32, (breadth, 3 * half), 0)
    col = lax.broadcasted_iota(jnp.int32, (breadth, 3 * half), 1)
    offset = (col >= half).astype(jnp.int32) + (col >= 2 * half).astype(jnp.int32)
    lane = col - offset * half
    odd = (lane >= half // 2).astype(jnp.int32)
    cell = 2 * (lane - odd * (half // 2)) + odd
    return jnp.where(row == 2 * cell + offset - 1, 1.0, 0.0).astype(BF16)


def place(dst, row, lanes, piece):
    c1 = piece(0).shape[0]
    for a in range(3):
        dst[row + a * c1 : row + (a + 1) * c1, lanes] = piece(a).astype(BF16)


def spread_layer(rows, pick, tall, turned, height, put):
    c1 = rows.shape[0] // height
    rows = rows.astype(F32)
    for part in range(tall.shape[0]):
        tall[part] = rows[:, part * 128 : (part + 1) * 128]
    for y in range(height):
        parts = [tall[part, pl.ds(y, c1, stride=height), :] for part in range(tall.shape[0])]
        turned[y * c1 : (y + 1) * c1, :] = jnp.concatenate(parts, axis=1).astype(BF16)
    cells = dot(turned[...], pick)
    mx = cells.shape[1] // 3
    for y in range(height):
        put(y, lambda a: cells[y * c1 : (y + 1) * c1, a * mx : (a + 1) * mx])


def by_parity(axis, run, pair, cross):
    odd = lax.rem(lax.axis_index(axis), 2)
    pl.when(odd == 1)(lambda: run(pair, cross))
    pl.when(odd == 0)(lambda: run(cross, pair))


def first_kernel(rims, pair, cross):
    count = pair.shape[0]

    def fill(down, up):
        up[...] = rims[:count]
        down[: rims.shape[0] - count] = rims[count:]

    by_parity("core", fill, pair, cross)


def edge_kernel(dims, vol, cot, z_pair, z_cross, pair, cross, below, above, tall):
    c1, depth, height, breadth = dims
    dz, dy, dx, c3 = cot.shape

    def take(from_below, from_above):
        below[...] = from_below[...].astype(F32)[:, height - 8 :]
        above[...] = from_above[: dx // height, :, :c3].reshape(dx, c3)

    by_parity("core", take, z_pair, z_cross)

    def fill(down, up):
        for z in range(depth + 1):
            top = vol[:, z - 1].astype(F32)[:, height - 8 :] if z else below[...]
            top = top.reshape(c1 * 8, breadth)
            for part in range(breadth // 128):
                lanes = slice(part * 128, (part + 1) * 128)
                slot = (z * (breadth // 128) + part) % 4
                tall[slot] = top[:, lanes]
                up[z * c1 : (z + 1) * c1, lanes] = tall[slot, pl.ds(7, c1, stride=8), :].astype(BF16)
        for z in range(dz):
            down[z * dx : (z + 1) * dx, :c3] = cot[z, 0]
        down[dz * dx : (dz + 1) * dx, :c3] = above[...]

    by_parity("gy", fill, pair, cross)


def gather_kernel(dims, vol, even, odd, tall, turned):
    c1, depth, height, breadth = dims
    mx = breadth // 2
    pick = picking_matrix(breadth)
    for layer in range(depth):
        rows = vol[:, layer].reshape(c1 * height, breadth)
        dst = even if layer % 2 else odd
        lanes = slice(layer // 2 * mx, (layer // 2 + 1) * mx)
        put = lambda y, piece: place(dst, y * 3 * c1, lanes, piece)
        spread_layer(rows, pick, tall.at[layer % 2], turned.at[layer % 2], height, put)


def silu_and_slope(pre):
    sigma = jax.nn.sigmoid(pre)
    return (pre * sigma).astype(BF16), sigma * (1.0 + pre * (1.0 - sigma))


def put_active(act, active, y, c2, dy, mx):
    for z in range(active.shape[1] // mx):
        cls = (z % 2) * 2 + y % 2
        at = (z // 2) * dy + y // 2
        act[cls * c2 : (cls + 1) * c2, at * mx : (at + 1) * mx] = active[:, z * mx : (z + 1) * mx]


def put_pair(pairs, top, here, last):
    dx = here.shape[0]
    zero = jnp.zeros_like(here)
    moved = jnp.where(last, 0.0, pltpu.roll(here.astype(F32), dx - 1, 0)).astype(BF16)
    pairs[top : top + dx, :] = jnp.concatenate([zero, here, zero], axis=1)
    pairs[top + dx : top + 2 * dx, :] = jnp.concatenate([moved, zero, here], axis=1)


def classes_of(sz, sy):
    classes = [(pz, py) for pz in range(2) for py in range(2) if pz >= sz and py >= sy]
    return classes, [(0 if sz else 1 + pz, 0 if sy else 1 + py) for pz, py in classes]


def filters_of(kd, taps):
    return jnp.concatenate(
        [jnp.concatenate([kd[(az * 3 + ay) * 3 + ax] for ax in range(3)], axis=1) for az, ay in taps], axis=0
    )


def window(even, odd, side, y, az, blk, mx):
    rows = slice((2 * y - 1) * blk, (2 * y + 2) * blk)
    if az == 0:
        return jnp.concatenate([side[2 * y * blk : (2 * y + 3) * blk, :], even[rows, : even.shape[1] - mx]], axis=1)
    return odd[rows, :] if az == 1 else even[rows, :]


def early_kernel(dims, even, odd, z_pair, z_cross, cot, km, kd, rim_z, act, slope, pairs, back, deep, mid, below, above, tall, turned, grad):
    c1, c2, c3, depth, height, breadth = dims
    mz, my, mx = depth // 2, height // 2, breadth // 2
    dz, dy, dx = mz // 2, my // 2, mx // 2
    blk = 3 * c1

    def take(from_below, from_above):
        below[...] = from_below[...].reshape(c1 * height, breadth)
        above[...] = from_above[: dy * dx // height, :, :c3].reshape(dy, dx, c3)

    by_parity("core", take, z_pair, z_cross)
    put = lambda y, piece: place(rim_z, (y + 1) * blk, slice(0, mx), piece)
    spread_layer(below[...], picking_matrix(breadth), tall, turned, height, put)
    turned_km = km[...].astype(F32).T.astype(BF16)
    put_active(act, jnp.zeros((c2, mz * mx), BF16), 0, c2, dy, mx)
    for y in range(1, my):
        cells = jnp.concatenate([window(even, odd, rim_z, y, az, blk, mx) for az in range(3)], axis=0)
        active, slope[y] = silu_and_slope(dot(turned_km, cells))
        put_active(act, active, y, c2, dy, mx)

    last = lax.broadcasted_iota(jnp.int32, (dx, c3), 0) == dx - 1
    for z in range(dz + 1):
        for y in range(dy):
            put_pair(pairs, (z * (dy + 1) + y) * mx, above[y] if z == dz else cot[z, y], last)

    for sz in range(2):
        for sy in range(2):
            classes, taps = classes_of(sz, sy)
            lhs = jnp.concatenate([act[(pz * 2 + py) * c2 : (pz * 2 + py + 1) * c2, :] for pz, py in classes], axis=0)
            filters = filters_of(kd, taps)
            total = None
            for z in range(dz):
                start, count = z * dy * mx, (dy - sy) * mx
                top = ((z + sz) * (dy + 1) + sy) * mx
                cells = pairs[top : top + count, :]
                term = dot(lhs[:, start : start + count], cells)
                total = term if total is None else total + term
                grads = dot(filters, cells, NT)
                for n, (pz, py) in enumerate(classes):
                    rows = slice((pz * 2 + py) * c2, (pz * 2 + py + 1) * c2)
                    piece = grads[n * c2 : (n + 1) * c2]
                    if sz or sy:
                        piece = piece + back[rows, start : start + count]
                    back[rows, start : start + count] = piece
            for n, (az, ay) in enumerate(taps):
                deep[az * 3 + ay] = total[n * c2 : (n + 1) * c2]

    for y in range(1, my - 1):
        put_grad(grad.at[y - 1], back, slope[y], y, c2, dy, mx)
    for az in range(3):
        total = None
        for y in range(1, my - 1):
            term = dot(window(even, odd, rim_z, y, az, blk, mx), grad[y - 1], NT)
            total = term if total is None else total + term
        mid[az] = total


def put_grad(dst, back, slope, y, c2, dy, mx):
    for z in range(dst.shape[1] // mx):
        cls = (z % 2) * 2 + y % 2
        at = (z // 2) * dy + y // 2
        value = back[cls * c2 : (cls + 1) * c2, at * mx : (at + 1) * mx] * slope[:, z * mx : (z + 1) * mx]
        dst[:, z * mx : (z + 1) * mx] = value.astype(BF16)


def main_kernel(dims, even, odd, rim_z, act, slope, pairs, back_in, deep_in, mid_in, y_pair, y_cross, km, kd, keep, send, beside, cot_beside, corner, rim_even, rim_odd, rim_pairs, back, grad, sums):
    c1, c2, c3, depth, height, breadth, n_pl, n_gy = dims
    mz, my, mx = depth // 2, height // 2, breadth // 2
    dz, dy, dx = mz // 2, my // 2, mx // 2
    pick = picking_matrix(breadth)
    blk = 3 * c1

    def take(from_below, from_above):
        beside[...] = from_below[...]
        cot_beside[...] = from_above[: (dz + 1) * dx, :c3]

    by_parity("gy", take, y_pair, y_cross)

    for layer in range(depth + 1):
        rim = dot(beside[layer * c1 : (layer + 1) * c1, :], pick)
        if layer == 0:
            dst, at = corner, 0
        else:
            dst, at = (rim_odd, layer // 2) if layer % 2 else (rim_even, layer // 2 - 1)
        place(dst, 0, slice(at * mx, (at + 1) * mx), lambda a: rim[:, a * mx : (a + 1) * mx])
    upper = jnp.concatenate([rim_even[...], even[: 2 * blk, :]], axis=0)
    side = jnp.concatenate([corner[...], rim_z[blk : 3 * blk, :]], axis=0)
    first = [
        jnp.concatenate([side, upper[:, : (mz - 1) * mx]], axis=1),
        jnp.concatenate([rim_odd[...], odd[: 2 * blk, :]], axis=0),
        upper,
    ]

    turned_km = km[...].astype(F32).T.astype(BF16)
    active, low_slope = silu_and_slope(dot(turned_km, jnp.concatenate(first, axis=0)))

    last = lax.broadcasted_iota(jnp.int32, (dx, c3), 0) == dx - 1
    for z in range(dz + 1):
        put_pair(rim_pairs, z * mx, cot_beside[z * dx : (z + 1) * dx, :], last)

    back[...] = back_in[...]
    deep = {(az, ay): deep_in[az * 3 + ay] for az in range(3) for ay in range(3)}
    for sz in range(2):
        for sy in range(2):
            group = [(c, t) for c, t in zip(*classes_of(sz, sy)) if c[1] == sy]
            filters = filters_of(kd, [tap for _, tap in group])
            for z in range(dz):
                lanes = slice((z * dy + dy - 1) * mx, (z * dy + dy) * mx)
                rows = [slice((pz * 2 + py) * c2, (pz * 2 + py + 1) * c2) for (pz, py), _ in group]
                if sy:
                    cells = rim_pairs[(z + sz) * mx : (z + sz + 1) * mx, :]
                    lhs = [act[r, lanes] for r in rows]
                    grads = dot(filters, cells, NT)
                    for n, r in enumerate(rows):
                        back[r, lanes] = back[r, lanes] + grads[n * c2 : (n + 1) * c2]
                else:
                    top = (z + sz) * (dy + 1) * mx
                    cells = pairs[top : top + mx, :]
                    lhs = [active[:, (2 * z + pz) * mx : (2 * z + pz + 1) * mx] for (pz, py), _ in group]
                term = dot(jnp.concatenate(lhs, axis=0), cells)
                for n, (_, tap) in enumerate(group):
                    deep[tap] = deep[tap] + term[n * c2 : (n + 1) * c2]
    deep = {
        (az * 3 + ay) * 3 + ax: deep[az, ay][:, ax * c3 : (ax + 1) * c3]
        for az in range(3) for ay in range(3) for ax in range(3)
    }

    put_grad(grad.at[0], back, low_slope, 0, c2, dy, mx)
    put_grad(grad.at[1], back, slope[my - 1], my - 1, c2, dy, mx)
    mids = []
    for az in range(3):
        upper_row = dot(window(even, odd, rim_z, my - 1, az, blk, mx), grad[1], NT)
        mids.append(mid_in[az] + dot(first[az], grad[0], NT) + upper_row)
    mid = jnp.concatenate(mids, axis=0)

    share = c3 // n_gy
    per = 448 // (2 * n_pl)
    chunk = (n_gy + 1) * per

    def spread(value, first, offset):
        done = 0
        while done < value.shape[0]:
            k, r = divmod(first + done, per)
            count = min(per - r, value.shape[0] - done)
            core, start = k % 2, k // 2 * chunk + offset + r
            sums[core, start : start + count, :] = value[done : done + count]
            done += count

    for slab in range(14):
        second = deep[2 * slab + 1] if 2 * slab + 1 < 27 else jnp.zeros((c2, c3), F32)
        turned = jnp.concatenate([deep[2 * slab], second], axis=0).T
        for g in range(n_gy):
            spread(turned[g * share : (g + 1) * share], slab * share, g * per)
    half = mid.shape[0] // 2
    packed = jnp.concatenate([mid[:half], mid[half:]], axis=1)
    packed = jnp.concatenate([packed, jnp.zeros((448 - half, 128), F32)], axis=0)
    spread(packed, 0, n_gy * per)
    core = lax.axis_index("core")
    keep[...] = sums[core]
    send[...] = sums[1 - core]


def last_kernel(dims, scales, got, mid_out, deep_out):
    n_all, share, c2, per = dims
    whole = got[...]
    deep = whole[:, :per].reshape(n_all * per, 128) * scales[1]
    mid = whole[:, per:].reshape(n_all * per, 128) * scales[0]
    for a in range(27):
        deep_out[a] = deep[(a // 2) * share : (a // 2 + 1) * share, (a % 2) * c2 : (a % 2 + 1) * c2]
    mid_out[:432] = mid[:432, :64]
    mid_out[432:] = mid[:432, 64:]


def on_device(volume, kernel_mid, kernel_deep, cotangent):
    n_dp = lax.axis_size("dp")
    gz = ("gx", "core")
    n_gz = lax.axis_size(gz)
    n_gy = lax.axis_size("gy")
    samples, c1, depth, height, breadth = volume.shape
    c2, c3 = kernel_mid.shape[0], kernel_deep.shape[0]
    count_mid = n_dp * samples * (n_gz * depth // 2) * (n_gy * height // 2) * (breadth // 2)
    count_deep = n_dp * samples * (n_gz * depth // 4) * (n_gy * height // 4) * (breadth // 4)
    mz, my, mx = depth // 2, height // 2, breadth // 2
    dz, dy, dx = mz // 2, my // 2, mx // 2
    n_pl = n_dp * n_gz // 2
    vol = volume[0]
    cot = cotangent[0].transpose(1, 2, 3, 0)
    in_vmem = pl.BlockSpec(memory_space=pltpu.VMEM)
    cot_layer = jnp.pad(cot[0].reshape(-1, height, c3), ((0, 0), (0, 0), (0, breadth - c3)))
    rims = jnp.concatenate([vol[:, -1], cot_layer], axis=0)
    payload = jax.ShapeDtypeStruct((c1, height, breadth), BF16)
    pair, cross = pl.pallas_call(
        first_kernel,
        out_shape=(payload, payload),
        in_specs=[in_vmem],
        out_specs=(in_vmem, in_vmem),
        compiler_params=pltpu.CompilerParams(vmem_limit_bytes=4 * 1024 * 1024),
    )(rims)
    z_cross = swapped(cross, gz, 1)
    z_pair = swapped(pair, gz, 0)
    blk = 3 * c1
    own_cells = jax.ShapeDtypeStruct((height * blk, mz * mx), BF16)
    even, odd = pl.pallas_call(
        functools.partial(gather_kernel, (c1, depth, height, breadth)),
        out_shape=(own_cells, own_cells),
        in_specs=[in_vmem],
        out_specs=(in_vmem, in_vmem),
        scratch_shapes=[
            pltpu.VMEM((2, breadth // 128, c1 * height, 128), F32),
            pltpu.VMEM((2, c1 * height, breadth), BF16),
        ],
        cost_estimate=pl.CostEstimate(flops=2 * c1 * depth * height * breadth * 3 * mx, bytes_accessed=8 << 20, transcendentals=0),
        compiler_params=pltpu.CompilerParams(vmem_limit_bytes=24 * 1024 * 1024),
    )(vol)
    payload = jax.ShapeDtypeStruct(((depth + 1) * c1, breadth), BF16)
    pair, cross = pl.pallas_call(
        functools.partial(edge_kernel, (c1, depth, height, breadth)),
        out_shape=(payload, payload),
        in_specs=[in_vmem] * 4,
        out_specs=(in_vmem, in_vmem),
        scratch_shapes=[
            pltpu.VMEM((c1, 8, breadth), F32),
            pltpu.VMEM((dx, c3), BF16),
            pltpu.VMEM((4, c1 * 8, 128), F32),
        ],
        compiler_params=pltpu.CompilerParams(vmem_limit_bytes=16 * 1024 * 1024),
    )(vol, cot, z_pair, z_cross)
    pair, cross, even, odd = lax.optimization_barrier((pair, cross, even, odd))
    y_pair, y_cross = swapped(pair, "gy", 0), swapped(cross, "gy", 1)
    km = kernel_mid.transpose(2, 3, 4, 1, 0).reshape(27 * c1, c2)
    kd = kernel_deep.transpose(2, 3, 4, 1, 0).reshape(27, c2, c3)

    share = c3 // n_gy
    per = 448 // (2 * n_pl)
    chunk = (n_gy + 1) * per
    rim_z, act, slope, pairs, back, deep, mid = pl.pallas_call(
        functools.partial(early_kernel, (c1, c2, c3, depth, height, breadth)),
        out_shape=(
            jax.ShapeDtypeStruct(((height + 1) * blk, mx), BF16),
            jax.ShapeDtypeStruct((4 * c2, dz * dy * mx), BF16),
            jax.ShapeDtypeStruct((my, c2, mz * mx), F32),
            jax.ShapeDtypeStruct(((dz + 1) * (dy + 1) * mx, 3 * c3), BF16),
            jax.ShapeDtypeStruct((4 * c2, dz * dy * mx), F32),
            jax.ShapeDtypeStruct((9, c2, 3 * c3), F32),
            jax.ShapeDtypeStruct((3, 3 * blk, c2), F32),
        ),
        in_specs=[in_vmem] * 7,
        out_specs=(in_vmem,) * 7,
        scratch_shapes=[
            pltpu.VMEM((c1 * height, breadth), BF16),
            pltpu.VMEM((dy, dx, c3), BF16),
            pltpu.VMEM((breadth // 128, c1 * height, 128), F32),
            pltpu.VMEM((c1 * height, breadth), BF16),
            pltpu.VMEM((my - 2, c2, mz * mx), BF16),
        ],
        cost_estimate=pl.CostEstimate(flops=2 * c1 * depth * height * breadth * 3 * mx, bytes_accessed=8 << 20, transcendentals=0),
        compiler_params=pltpu.CompilerParams(vmem_limit_bytes=24 * 1024 * 1024),
    )(even, odd, z_pair, z_cross, cot, km, kd)
    keep, send = pl.pallas_call(
        functools.partial(main_kernel, (c1, c2, c3, depth, height, breadth, n_pl, n_gy)),
        out_shape=(jax.ShapeDtypeStruct((n_pl * chunk, 128), F32), jax.ShapeDtypeStruct((n_pl * chunk, 128), F32)),
        in_specs=[in_vmem] * 13,
        out_specs=(in_vmem, in_vmem),
        scratch_shapes=[
            pltpu.VMEM(((depth + 1) * c1, breadth), BF16),
            pltpu.VMEM(((dz + 1) * dx, c3), BF16),
            pltpu.VMEM((blk, mx), BF16),
            pltpu.VMEM((blk, mz * mx), BF16),
            pltpu.VMEM((blk, mz * mx), BF16),
            pltpu.VMEM(((dz + 1) * mx, 3 * c3), BF16),
            pltpu.VMEM((4 * c2, dz * dy * mx), F32),
            pltpu.VMEM((2, c2, mz * mx), BF16),
            pltpu.VMEM((2, n_pl * chunk, 128), F32),
        ],
        compiler_params=pltpu.CompilerParams(vmem_limit_bytes=32 * 1024 * 1024),
    )(even, odd, rim_z, act, slope, pairs, back, deep, mid, y_pair, y_cross, km, kd)
    other = lax.ppermute(send, "core", [(0, 1), (1, 0)])
    pair = (keep + other).astype(BF16).reshape(n_pl, chunk, 128)
    own = jnp.sum(lax.all_to_all(pair, ("dp", "gx"), 0, 0).astype(F32), axis=0)
    deep_own = own[: n_gy * per].reshape(n_gy, per, 128)
    mid_own = jnp.broadcast_to(own[n_gy * per :], (n_gy, per, 128))
    column = jnp.concatenate([deep_own, mid_own], axis=1).astype(BF16)
    own = jnp.sum(lax.all_to_all(column, "gy", 0, 0).astype(F32), axis=0)
    whole = lax.all_gather(own, ("dp", "gx", "core"), axis=0)
    scales = (1.0 / math.sqrt(count_mid), 1.0 / math.sqrt(count_deep))
    mid, deep = pl.pallas_call(
        functools.partial(last_kernel, (2 * n_pl, share, c2, per), scales),
        out_shape=(jax.ShapeDtypeStruct((27 * c1, c2), F32), jax.ShapeDtypeStruct((27, share, c2), F32)),
        in_specs=[in_vmem],
        out_specs=(in_vmem, in_vmem),
        compiler_params=pltpu.CompilerParams(vmem_limit_bytes=24 * 1024 * 1024),
    )(whole)
    mid = mid.reshape(3, 3, 3, c1, c2).transpose(4, 3, 0, 1, 2)
    deep = deep.reshape(3, 3, 3, share, c2).transpose(3, 4, 0, 1, 2)
    return mid, deep


def solution(mesh):
    n_dp, n_gz, n_gy = (mesh.shape[name] for name in ("dp", "gz", "gy"))
    split = Mesh(mesh.devices.reshape(n_dp, n_gz // 2, 2, n_gy), ("dp", "gx", "core", "gy"))
    by_cells = P("dp", None, ("gx", "core"), "gy", None)
    in_specs = (by_cells, P(), P(), by_cells)
    out_specs = (P(), P("gy", None, None, None, None))
    return jax.shard_map(
        on_device, mesh=split, in_specs=in_specs, out_specs=out_specs, check_vma=False
    )
```

```python
import functools
import math

import jax
import jax.numpy as jnp
from jax import lax
from jax.experimental import pallas as pl
from jax.experimental.pallas import tpu as pltpu
from jax.sharding import Mesh, PartitionSpec as P

BF16 = jnp.bfloat16
F32 = jnp.float32
NN = (((1,), (0,)), ((), ()))
NT = (((1,), (1,)), ((), ()))


def dot(a, b, dims=NN):
    return lax.dot_general(a, b, dims, preferred_element_type=F32)


def swapped(block, axis, first):
    count = lax.axis_size(axis)
    route = [(i, i + 1) for i in range(first, count - 1, 2)]
    return lax.ppermute(block, axis, route + [(j, i) for i, j in route])


def picking_matrix(breadth):
    half = breadth // 2
    row = lax.broadcasted_iota(jnp.int32, (breadth, 3 * half), 0)
    col = lax.broadcasted_iota(jnp.int32, (breadth, 3 * half), 1)
    offset = (col >= half).astype(jnp.int32) + (col >= 2 * half).astype(jnp.int32)
    lane = col - offset * half
    odd = (lane >= half // 2).astype(jnp.int32)
    cell = 2 * (lane - odd * (half // 2)) + odd
    return jnp.where(row == 2 * cell + offset - 1, 1.0, 0.0).astype(BF16)


def place(dst, row, lanes, piece):
    c1 = piece(0).shape[0]
    for a in range(3):
        dst[row + a * c1 : row + (a + 1) * c1, lanes] = piece(a).astype(BF16)


def spread_layer(rows, pick, tall, turned, height, put):
    c1 = rows.shape[0] // height
    rows = rows.astype(F32)
    for part in range(tall.shape[0]):
        tall[part] = rows[:, part * 128 : (part + 1) * 128]
    for y in range(height):
        parts = [tall[part, pl.ds(y, c1, stride=height), :] for part in range(tall.shape[0])]
        turned[y * c1 : (y + 1) * c1, :] = jnp.concatenate(parts, axis=1).astype(BF16)
    cells = dot(turned[...], pick)
    mx = cells.shape[1] // 3
    for y in range(height):
        put(y, lambda a: cells[y * c1 : (y + 1) * c1, a * mx : (a + 1) * mx])


def by_parity(axis, run, pair, cross):
    odd = lax.rem(lax.axis_index(axis), 2)
    pl.when(odd == 1)(lambda: run(pair, cross))
    pl.when(odd == 0)(lambda: run(cross, pair))


def edge_kernel(dims, vol, cot, z_pair, z_cross, pair, cross, below, above, tall):
    c1, depth, height, breadth = dims
    dz, dy, dx, c3 = cot.shape

    def take(from_below, from_above):
        below[...] = from_below[...].astype(F32)[:, height - 8 :]
        above[...] = from_above[: dx // height, :, :c3].reshape(dx, c3)

    by_parity("core", take, z_pair, z_cross)

    def fill(down, up):
        for z in range(depth + 1):
            top = vol[:, z - 1].astype(F32)[:, height - 8 :] if z else below[...]
            top = top.reshape(c1 * 8, breadth)
            for part in range(breadth // 128):
                lanes = slice(part * 128, (part + 1) * 128)
                slot = (z * (breadth // 128) + part) % 4
                tall[slot] = top[:, lanes]
                up[z * c1 : (z + 1) * c1, lanes] = tall[slot, pl.ds(7, c1, stride=8), :].astype(BF16)
        for z in range(dz):
            down[z * dx : (z + 1) * dx, :c3] = cot[z, 0]
        down[dz * dx : (dz + 1) * dx, :c3] = above[...]

    by_parity("gy", fill, pair, cross)


def gather_kernel(dims, vol, even, odd, tall, turned):
    c1, depth, height, breadth = dims
    mx = breadth // 2
    pick = picking_matrix(breadth)
    for layer in range(depth):
        rows = vol[:, layer].reshape(c1 * height, breadth)
        dst = even if layer % 2 else odd
        lanes = slice(layer // 2 * mx, (layer // 2 + 1) * mx)
        put = lambda y, piece: place(dst, y * 3 * c1, lanes, piece)
        spread_layer(rows, pick, tall.at[layer % 2], turned.at[layer % 2], height, put)


def silu_and_slope(pre):
    sigma = jax.nn.sigmoid(pre)
    return (pre * sigma).astype(BF16), sigma * (1.0 + pre * (1.0 - sigma))


def put_active(act, active, y, c2, dy, mx):
    for z in range(active.shape[1] // mx):
        cls = (z % 2) * 2 + y % 2
        at = (z // 2) * dy + y // 2
        act[cls * c2 : (cls + 1) * c2, at * mx : (at + 1) * mx] = active[:, z * mx : (z + 1) * mx]


def put_pair(pairs, top, here, last):
    dx = here.shape[0]
    zero = jnp.zeros_like(here)
    moved = jnp.where(last, 0.0, pltpu.roll(here.astype(F32), dx - 1, 0)).astype(BF16)
    pairs[top : top + dx, :] = jnp.concatenate([zero, here, zero], axis=1)
    pairs[top + dx : top + 2 * dx, :] = jnp.concatenate([moved, zero, here], axis=1)


def classes_of(sz, sy):
    classes = [(pz, py) for pz in range(2) for py in range(2) if pz >= sz and py >= sy]
    return classes, [(0 if sz else 1 + pz, 0 if sy else 1 + py) for pz, py in classes]


def filters_of(kd, taps):
    return jnp.concatenate(
        [jnp.concatenate([kd[(az * 3 + ay) * 3 + ax] for ax in range(3)], axis=1) for az, ay in taps], axis=0
    )


def window(even, odd, side, y, az, blk, mx):
    rows = slice((2 * y - 1) * blk, (2 * y + 2) * blk)
    if az == 0:
        return jnp.concatenate([side[2 * y * blk : (2 * y + 3) * blk, :], even[rows, : even.shape[1] - mx]], axis=1)
    return odd[rows, :] if az == 1 else even[rows, :]


def early_kernel(dims, even, odd, z_pair, z_cross, cot, km, kd, rim_z, act, slope, pairs, back, deep, mid, below, above, tall, turned, grad):
    c1, c2, c3, depth, height, breadth = dims
    mz, my, mx = depth // 2, height // 2, breadth // 2
    dz, dy, dx = mz // 2, my // 2, mx // 2
    blk = 3 * c1

    def take(from_below, from_above):
        below[...] = from_below[...].reshape(c1 * height, breadth)
        above[...] = from_above[: dy * dx // height, :, :c3].reshape(dy, dx, c3)

    by_parity("core", take, z_pair, z_cross)
    put = lambda y, piece: place(rim_z, (y + 1) * blk, slice(0, mx), piece)
    spread_layer(below[...], picking_matrix(breadth), tall, turned, height, put)
    turned_km = km[...].astype(F32).T.astype(BF16)
    put_active(act, jnp.zeros((c2, mz * mx), BF16), 0, c2, dy, mx)
    for y in range(1, my):
        cells = jnp.concatenate([window(even, odd, rim_z, y, az, blk, mx) for az in range(3)], axis=0)
        active, slope[y] = silu_and_slope(dot(turned_km, cells))
        put_active(act, active, y, c2, dy, mx)

    last = lax.broadcasted_iota(jnp.int32, (dx, c3), 0) == dx - 1
    for z in range(dz + 1):
        for y in range(dy):
            put_pair(pairs, (z * (dy + 1) + y) * mx, above[y] if z == dz else cot[z, y], last)

    for sz in range(2):
        for sy in range(2):
            classes, taps = classes_of(sz, sy)
            lhs = jnp.concatenate([act[(pz * 2 + py) * c2 : (pz * 2 + py + 1) * c2, :] for pz, py in classes], axis=0)
            filters = filters_of(kd, taps)
            total = None
            for z in range(dz):
                start, count = z * dy * mx, (dy - sy) * mx
                top = ((z + sz) * (dy + 1) + sy) * mx
                cells = pairs[top : top + count, :]
                term = dot(lhs[:, start : start + count], cells)
                total = term if total is None else total + term
                grads = dot(filters, cells, NT)
                for n, (pz, py) in enumerate(classes):
                    rows = slice((pz * 2 + py) * c2, (pz * 2 + py + 1) * c2)
                    piece = grads[n * c2 : (n + 1) * c2]
                    if sz or sy:
                        piece = piece + back[rows, start : start + count]
                    back[rows, start : start + count] = piece
            for n, (az, ay) in enumerate(taps):
                deep[az * 3 + ay] = total[n * c2 : (n + 1) * c2]

    for y in range(1, my - 1):
        put_grad(grad.at[y - 1], back, slope[y], y, c2, dy, mx)
    for az in range(3):
        total = None
        for y in range(1, my - 1):
            term = dot(window(even, odd, rim_z, y, az, blk, mx), grad[y - 1], NT)
            total = term if total is None else total + term
        mid[az] = total


def put_grad(dst, back, slope, y, c2, dy, mx):
    for z in range(dst.shape[1] // mx):
        cls = (z % 2) * 2 + y % 2
        at = (z // 2) * dy + y // 2
        value = back[cls * c2 : (cls + 1) * c2, at * mx : (at + 1) * mx] * slope[:, z * mx : (z + 1) * mx]
        dst[:, z * mx : (z + 1) * mx] = value.astype(BF16)


def main_kernel(dims, even, odd, rim_z, act, slope, pairs, back_in, deep_in, mid_in, y_cross, y_pair, km, kd, keep, send, beside, cot_beside, corner, rim_even, rim_odd, rim_pairs, back, grad, sums):
    c1, c2, c3, depth, height, breadth, n_pl, n_gy = dims
    mz, my, mx = depth // 2, height // 2, breadth // 2
    dz, dy, dx = mz // 2, my // 2, mx // 2
    pick = picking_matrix(breadth)
    blk = 3 * c1

    def take(from_below, from_above):
        beside[...] = from_below[...]
        cot_beside[...] = from_above[: (dz + 1) * dx, :c3]

    by_parity("gy", take, y_pair, y_cross)

    for layer in range(depth + 1):
        rim = dot(beside[layer * c1 : (layer + 1) * c1, :], pick)
        if layer == 0:
            dst, at = corner, 0
        else:
            dst, at = (rim_odd, layer // 2) if layer % 2 else (rim_even, layer // 2 - 1)
        place(dst, 0, slice(at * mx, (at + 1) * mx), lambda a: rim[:, a * mx : (a + 1) * mx])
    upper = jnp.concatenate([rim_even[...], even[: 2 * blk, :]], axis=0)
    side = jnp.concatenate([corner[...], rim_z[blk : 3 * blk, :]], axis=0)
    first = [
        jnp.concatenate([side, upper[:, : (mz - 1) * mx]], axis=1),
        jnp.concatenate([rim_odd[...], odd[: 2 * blk, :]], axis=0),
        upper,
    ]

    turned_km = km[...].astype(F32).T.astype(BF16)
    active, low_slope = silu_and_slope(dot(turned_km, jnp.concatenate(first, axis=0)))

    last = lax.broadcasted_iota(jnp.int32, (dx, c3), 0) == dx - 1
    for z in range(dz + 1):
        put_pair(rim_pairs, z * mx, cot_beside[z * dx : (z + 1) * dx, :], last)

    back[...] = back_in[...]
    deep = {(az, ay): deep_in[az * 3 + ay] for az in range(3) for ay in range(3)}
    for sz in range(2):
        for sy in range(2):
            group = [(c, t) for c, t in zip(*classes_of(sz, sy)) if c[1] == sy]
            filters = filters_of(kd, [tap for _, tap in group])
            for z in range(dz):
                lanes = slice((z * dy + dy - 1) * mx, (z * dy + dy) * mx)
                rows = [slice((pz * 2 + py) * c2, (pz * 2 + py + 1) * c2) for (pz, py), _ in group]
                if sy:
                    cells = rim_pairs[(z + sz) * mx : (z + sz + 1) * mx, :]
                    lhs = [act[r, lanes] for r in rows]
                    grads = dot(filters, cells, NT)
                    for n, r in enumerate(rows):
                        back[r, lanes] = back[r, lanes] + grads[n * c2 : (n + 1) * c2]
                else:
                    top = (z + sz) * (dy + 1) * mx
                    cells = pairs[top : top + mx, :]
                    lhs = [active[:, (2 * z + pz) * mx : (2 * z + pz + 1) * mx] for (pz, py), _ in group]
                term = dot(jnp.concatenate(lhs, axis=0), cells)
                for n, (_, tap) in enumerate(group):
                    deep[tap] = deep[tap] + term[n * c2 : (n + 1) * c2]
    deep = {
        (az * 3 + ay) * 3 + ax: deep[az, ay][:, ax * c3 : (ax + 1) * c3]
        for az in range(3) for ay in range(3) for ax in range(3)
    }

    put_grad(grad.at[0], back, low_slope, 0, c2, dy, mx)
    put_grad(grad.at[1], back, slope[my - 1], my - 1, c2, dy, mx)
    mids = []
    for az in range(3):
        upper_row = dot(window(even, odd, rim_z, my - 1, az, blk, mx), grad[1], NT)
        mids.append(mid_in[az] + dot(first[az], grad[0], NT) + upper_row)
    mid = jnp.concatenate(mids, axis=0)

    share = c3 // n_gy
    per = 448 // (2 * n_pl)
    chunk = (n_gy + 1) * per

    def spread(value, first, offset):
        done = 0
        while done < value.shape[0]:
            k, r = divmod(first + done, per)
            count = min(per - r, value.shape[0] - done)
            core, start = k % 2, k // 2 * chunk + offset + r
            sums[core, start : start + count, :] = value[done : done + count]
            done += count

    for slab in range(14):
        second = deep[2 * slab + 1] if 2 * slab + 1 < 27 else jnp.zeros((c2, c3), F32)
        turned = jnp.concatenate([deep[2 * slab], second], axis=0).T
        for g in range(n_gy):
            spread(turned[g * share : (g + 1) * share], slab * share, g * per)
    half = mid.shape[0] // 2
    packed = jnp.concatenate([mid[:half], mid[half:]], axis=1)
    packed = jnp.concatenate([packed, jnp.zeros((448 - half, 128), F32)], axis=0)
    spread(packed, 0, n_gy * per)
    core = lax.axis_index("core")
    keep[...] = sums[core]
    send[...] = sums[1 - core]


def last_kernel(dims, scales, got, mid_out, deep_out):
    n_all, share, c2, per = dims
    whole = got[...]
    deep = whole[:, :per].reshape(n_all * per, 128) * scales[1]
    mid = whole[:, per:].reshape(n_all * per, 128) * scales[0]
    for a in range(27):
        deep_out[a] = deep[(a // 2) * share : (a // 2 + 1) * share, (a % 2) * c2 : (a % 2 + 1) * c2]
    mid_out[:432] = mid[:432, :64]
    mid_out[432:] = mid[:432, 64:]


def on_device(volume, kernel_mid, kernel_deep, cotangent):
    n_dp = lax.axis_size("dp")
    gz = ("gx", "core")
    n_gz = lax.axis_size(gz)
    n_gy = lax.axis_size("gy")
    samples, c1, depth, height, breadth = volume.shape
    c2, c3 = kernel_mid.shape[0], kernel_deep.shape[0]
    count_mid = n_dp * samples * (n_gz * depth // 2) * (n_gy * height // 2) * (breadth // 2)
    count_deep = n_dp * samples * (n_gz * depth // 4) * (n_gy * height // 4) * (breadth // 4)
    mz, my, mx = depth // 2, height // 2, breadth // 2
    dz, dy, dx = mz // 2, my // 2, mx // 2
    n_pl = n_dp * n_gz // 2
    vol = volume[0]
    cot = cotangent[0].transpose(1, 2, 3, 0)
    in_vmem = pl.BlockSpec(memory_space=pltpu.VMEM)
    layer = vol.reshape(c1, depth * height, breadth)[:, -height:]
    flat = cot.reshape(-1, height, c3)
    cot_layer = jnp.pad(flat, ((0, c1 - flat.shape[0]), (0, 0), (0, breadth - c3)))
    odd = lax.axis_index("core") == 1
    cross, pair = jnp.where(odd, layer, cot_layer), jnp.where(odd, cot_layer, layer)
    z_cross = swapped(cross, gz, 1)
    z_pair = swapped(pair, gz, 0)
    blk = 3 * c1
    own_cells = jax.ShapeDtypeStruct((height * blk, mz * mx), BF16)
    even, odd = pl.pallas_call(
        functools.partial(gather_kernel, (c1, depth, height, breadth)),
        out_shape=(own_cells, own_cells),
        in_specs=[in_vmem],
        out_specs=(in_vmem, in_vmem),
        scratch_shapes=[
            pltpu.VMEM((2, breadth // 128, c1 * height, 128), F32),
            pltpu.VMEM((2, c1 * height, breadth), BF16),
        ],
        cost_estimate=pl.CostEstimate(flops=2 * c1 * depth * height * breadth * 3 * mx, bytes_accessed=8 << 20, transcendentals=0),
        compiler_params=pltpu.CompilerParams(vmem_limit_bytes=24 * 1024 * 1024),
    )(vol)
    payload = jax.ShapeDtypeStruct(((depth + 1) * c1, breadth), BF16)
    pair, cross = pl.pallas_call(
        functools.partial(edge_kernel, (c1, depth, height, breadth)),
        out_shape=(payload, payload),
        in_specs=[in_vmem] * 4,
        out_specs=(in_vmem, in_vmem),
        scratch_shapes=[
            pltpu.VMEM((c1, 8, breadth), F32),
            pltpu.VMEM((dx, c3), BF16),
            pltpu.VMEM((4, c1 * 8, 128), F32),
        ],
        compiler_params=pltpu.CompilerParams(vmem_limit_bytes=16 * 1024 * 1024),
    )(vol, cot, z_pair, z_cross)
    pair, cross, even, odd = lax.optimization_barrier((pair, cross, even, odd))
    y_pair, y_cross = swapped(pair, "gy", 0), swapped(cross, "gy", 1)
    km = kernel_mid.transpose(2, 3, 4, 1, 0).reshape(27 * c1, c2)
    kd = kernel_deep.transpose(2, 3, 4, 1, 0).reshape(27, c2, c3)

    share = c3 // n_gy
    per = 448 // (2 * n_pl)
    chunk = (n_gy + 1) * per
    rim_z, act, slope, pairs, back, deep, mid = pl.pallas_call(
        functools.partial(early_kernel, (c1, c2, c3, depth, height, breadth)),
        out_shape=(
            jax.ShapeDtypeStruct(((height + 1) * blk, mx), BF16),
            jax.ShapeDtypeStruct((4 * c2, dz * dy * mx), BF16),
            jax.ShapeDtypeStruct((my, c2, mz * mx), F32),
            jax.ShapeDtypeStruct(((dz + 1) * (dy + 1) * mx, 3 * c3), BF16),
            jax.ShapeDtypeStruct((4 * c2, dz * dy * mx), F32),
            jax.ShapeDtypeStruct((9, c2, 3 * c3), F32),
            jax.ShapeDtypeStruct((3, 3 * blk, c2), F32),
        ),
        in_specs=[in_vmem] * 7,
        out_specs=(in_vmem,) * 7,
        scratch_shapes=[
            pltpu.VMEM((c1 * height, breadth), BF16),
            pltpu.VMEM((dy, dx, c3), BF16),
            pltpu.VMEM((breadth // 128, c1 * height, 128), F32),
            pltpu.VMEM((c1 * height, breadth), BF16),
            pltpu.VMEM((my - 2, c2, mz * mx), BF16),
        ],
        cost_estimate=pl.CostEstimate(flops=2 * c1 * depth * height * breadth * 3 * mx, bytes_accessed=8 << 20, transcendentals=0),
        compiler_params=pltpu.CompilerParams(vmem_limit_bytes=24 * 1024 * 1024),
    )(even, odd, z_pair, z_cross, cot, km, kd)
    keep, send = pl.pallas_call(
        functools.partial(main_kernel, (c1, c2, c3, depth, height, breadth, n_pl, n_gy)),
        out_shape=(jax.ShapeDtypeStruct((n_pl * chunk, 128), F32), jax.ShapeDtypeStruct((n_pl * chunk, 128), F32)),
        in_specs=[in_vmem] * 13,
        out_specs=(in_vmem, in_vmem),
        scratch_shapes=[
            pltpu.VMEM(((depth + 1) * c1, breadth), BF16),
            pltpu.VMEM(((dz + 1) * dx, c3), BF16),
            pltpu.VMEM((blk, mx), BF16),
            pltpu.VMEM((blk, mz * mx), BF16),
            pltpu.VMEM((blk, mz * mx), BF16),
            pltpu.VMEM(((dz + 1) * mx, 3 * c3), BF16),
            pltpu.VMEM((4 * c2, dz * dy * mx), F32),
            pltpu.VMEM((2, c2, mz * mx), BF16),
            pltpu.VMEM((2, n_pl * chunk, 128), F32),
        ],
        compiler_params=pltpu.CompilerParams(vmem_limit_bytes=32 * 1024 * 1024),
    )(even, odd, rim_z, act, slope, pairs, back, deep, mid, y_cross, y_pair, km, kd)
    other = lax.ppermute(send, "core", [(0, 1), (1, 0)])
    pair = (keep + other).astype(BF16).reshape(n_pl, chunk, 128)
    own = jnp.sum(lax.all_to_all(pair, ("dp", "gx"), 0, 0).astype(F32), axis=0)
    deep_own = own[: n_gy * per].reshape(n_gy, per, 128)
    mid_own = jnp.broadcast_to(own[n_gy * per :], (n_gy, per, 128))
    column = jnp.concatenate([deep_own, mid_own], axis=1).astype(BF16)
    own = jnp.sum(lax.all_to_all(column, "gy", 0, 0).astype(F32), axis=0)
    whole = lax.all_gather(own, ("dp", "gx", "core"), axis=0)
    scales = (1.0 / math.sqrt(count_mid), 1.0 / math.sqrt(count_deep))
    mid, deep = pl.pallas_call(
        functools.partial(last_kernel, (2 * n_pl, share, c2, per), scales),
        out_shape=(jax.ShapeDtypeStruct((27 * c1, c2), F32), jax.ShapeDtypeStruct((27, share, c2), F32)),
        in_specs=[in_vmem],
        out_specs=(in_vmem, in_vmem),
        compiler_params=pltpu.CompilerParams(vmem_limit_bytes=24 * 1024 * 1024),
    )(whole)
    mid = mid.reshape(3, 3, 3, c1, c2).transpose(4, 3, 0, 1, 2)
    deep = deep.reshape(3, 3, 3, share, c2).transpose(3, 4, 0, 1, 2)
    return mid, deep


def solution(mesh):
    n_dp, n_gz, n_gy = (mesh.shape[name] for name in ("dp", "gz", "gy"))
    split = Mesh(mesh.devices.reshape(n_dp, n_gz // 2, 2, n_gy), ("dp", "gx", "core", "gy"))
    by_cells = P("dp", None, ("gx", "core"), "gy", None)
    in_specs = (by_cells, P(), P(), by_cells)
    out_specs = (P(), P("gy", None, None, None, None))
    return jax.shard_map(
        on_device, mesh=split, in_specs=in_specs, out_specs=out_specs, check_vma=False
    )
```

```python
import functools
import math

import jax
import jax.numpy as jnp
from jax import lax
from jax.experimental import pallas as pl
from jax.experimental.pallas import tpu as pltpu
from jax.sharding import Mesh, PartitionSpec as P

BF16 = jnp.bfloat16
F32 = jnp.float32
NN = (((1,), (0,)), ((), ()))
NT = (((1,), (1,)), ((), ()))


def dot(a, b, dims=NN):
    return lax.dot_general(a, b, dims, preferred_element_type=F32)


def swapped(block, axis, first):
    count = lax.axis_size(axis)
    route = [(i, i + 1) for i in range(first, count - 1, 2)]
    return lax.ppermute(block, axis, route + [(j, i) for i, j in route])


def picking_matrix(breadth):
    half = breadth // 2
    row = lax.broadcasted_iota(jnp.int32, (breadth, 3 * half), 0)
    col = lax.broadcasted_iota(jnp.int32, (breadth, 3 * half), 1)
    offset = (col >= half).astype(jnp.int32) + (col >= 2 * half).astype(jnp.int32)
    lane = col - offset * half
    odd = (lane >= half // 2).astype(jnp.int32)
    cell = 2 * (lane - odd * (half // 2)) + odd
    return jnp.where(row == 2 * cell + offset - 1, 1.0, 0.0).astype(BF16)


def place(dst, row, lanes, piece):
    c1 = piece(0).shape[0]
    for a in range(3):
        dst[row + a * c1 : row + (a + 1) * c1, lanes] = piece(a).astype(BF16)


def spread_layer(rows, pick, tall, turned, height, put):
    c1 = rows.shape[0] // height
    rows = rows.astype(F32)
    for part in range(tall.shape[0]):
        tall[part] = rows[:, part * 128 : (part + 1) * 128]
    for y in range(height):
        parts = [tall[part, pl.ds(y, c1, stride=height), :] for part in range(tall.shape[0])]
        turned[y * c1 : (y + 1) * c1, :] = jnp.concatenate(parts, axis=1).astype(BF16)
    cells = dot(turned[...], pick)
    mx = cells.shape[1] // 3
    for y in range(height):
        put(y, lambda a: cells[y * c1 : (y + 1) * c1, a * mx : (a + 1) * mx])


def by_parity(axis, run, pair, cross):
    odd = lax.rem(lax.axis_index(axis), 2)
    pl.when(odd == 1)(lambda: run(pair, cross))
    pl.when(odd == 0)(lambda: run(cross, pair))


def edge_kernel(dims, vol, cot, z_pair, z_cross, pair, cross, below, above, tall):
    c1, depth, height, breadth = dims
    dz, dy, dx, c3 = cot.shape

    def take(from_below, from_above):
        below[...] = from_below[...].astype(F32)[:, height - 8 :]
        above[...] = from_above[: dx // height, :, :c3].reshape(dx, c3)

    by_parity("core", take, z_pair, z_cross)

    def fill(down, up):
        for z in range(depth + 1):
            top = vol[:, z - 1].astype(F32)[:, height - 8 :] if z else below[...]
            top = top.reshape(c1 * 8, breadth)
            for part in range(breadth // 128):
                lanes = slice(part * 128, (part + 1) * 128)
                slot = (z * (breadth // 128) + part) % 4
                tall[slot] = top[:, lanes]
                up[z * c1 : (z + 1) * c1, lanes] = tall[slot, pl.ds(7, c1, stride=8), :].astype(BF16)
        for z in range(dz):
            down[z * dx : (z + 1) * dx, :c3] = cot[z, 0]
        down[dz * dx : (dz + 1) * dx, :c3] = above[...]

    by_parity("gy", fill, pair, cross)


def gather_kernel(dims, vol, even, odd, tall, turned):
    c1, depth, height, breadth = dims
    mx = breadth // 2
    pick = picking_matrix(breadth)
    for layer in range(depth):
        rows = vol[:, layer].reshape(c1 * height, breadth)
        dst = even if layer % 2 else odd
        lanes = slice(layer // 2 * mx, (layer // 2 + 1) * mx)
        put = lambda y, piece: place(dst, y * 3 * c1, lanes, piece)
        spread_layer(rows, pick, tall.at[layer % 2], turned.at[layer % 2], height, put)


def back_kernel(cot, kd, order, pairs, back):
    dz, dy, dx, c3 = cot.shape
    c2, mx = kd.shape[1], 2 * dx
    last = lax.broadcasted_iota(jnp.int32, (dx, c3), 0) == dx - 1
    for z in range(dz):
        for y in range(dy):
            put_pair(pairs, (z * dy + y) * mx, cot[z, y], last)
    for sy in range(2):
        classes, taps = classes_of(0, sy)
        filters = filters_of(kd, taps)
        for z in range(dz):
            start, count = z * dy * mx, (dy - sy) * mx
            add_grads(back, dot(filters, pairs[start + sy * mx : start + dy * mx, :], NT), classes, start, count, c2, sy)


def add_grads(back, grads, classes, start, count, c2, held):
    for n, (pz, py) in enumerate(classes):
        rows = slice((pz * 2 + py) * c2, (pz * 2 + py + 1) * c2)
        piece = grads[n * c2 : (n + 1) * c2]
        if held:
            piece = piece + back[rows, start : start + count]
        back[rows, start : start + count] = piece


def silu_and_slope(pre):
    sigma = jax.nn.sigmoid(pre)
    return (pre * sigma).astype(BF16), sigma * (1.0 + pre * (1.0 - sigma))


def put_active(act, active, y, c2, dy, mx):
    for z in range(active.shape[1] // mx):
        cls = (z % 2) * 2 + y % 2
        at = (z // 2) * dy + y // 2
        act[cls * c2 : (cls + 1) * c2, at * mx : (at + 1) * mx] = active[:, z * mx : (z + 1) * mx]


def put_pair(pairs, top, here, last):
    dx = here.shape[0]
    zero = jnp.zeros_like(here)
    moved = jnp.where(last, 0.0, pltpu.roll(here.astype(F32), dx - 1, 0)).astype(BF16)
    pairs[top : top + dx, :] = jnp.concatenate([zero, here, zero], axis=1)
    pairs[top + dx : top + 2 * dx, :] = jnp.concatenate([moved, zero, here], axis=1)


def classes_of(sz, sy):
    classes = [(pz, py) for pz in range(2) for py in range(2) if pz >= sz and py >= sy]
    return classes, [(0 if sz else 1 + pz, 0 if sy else 1 + py) for pz, py in classes]


def filters_of(kd, taps):
    return jnp.concatenate(
        [jnp.concatenate([kd[(az * 3 + ay) * 3 + ax] for ax in range(3)], axis=1) for az, ay in taps], axis=0
    )


def window(even, odd, side, y, az, blk, mx):
    rows = slice((2 * y - 1) * blk, (2 * y + 2) * blk)
    if az == 0:
        return jnp.concatenate([side[2 * y * blk : (2 * y + 3) * blk, :], even[rows, : even.shape[1] - mx]], axis=1)
    return odd[rows, :] if az == 1 else even[rows, :]


def early_kernel(dims, even, odd, pairs, back_in, z_pair, z_cross, km, kd, rim_z, act, slope, pairs_above, back, deep, mid, below, above, tall, turned, grad):
    c1, c2, c3, depth, height, breadth = dims
    mz, my, mx = depth // 2, height // 2, breadth // 2
    dz, dy, dx = mz // 2, my // 2, mx // 2
    blk = 3 * c1

    def take(from_below, from_above):
        below[...] = from_below[...].reshape(c1 * height, breadth)
        above[...] = from_above[: dy * dx // height, :, :c3].reshape(dy, dx, c3)

    by_parity("core", take, z_pair, z_cross)
    put = lambda y, piece: place(rim_z, (y + 1) * blk, slice(0, mx), piece)
    spread_layer(below[...], picking_matrix(breadth), tall, turned, height, put)
    turned_km = km[...].astype(F32).T.astype(BF16)
    put_active(act, jnp.zeros((c2, mz * mx), BF16), 0, c2, dy, mx)
    for y in range(1, my):
        cells = jnp.concatenate([window(even, odd, rim_z, y, az, blk, mx) for az in range(3)], axis=0)
        active, slope[y] = silu_and_slope(dot(turned_km, cells))
        put_active(act, active, y, c2, dy, mx)

    last = lax.broadcasted_iota(jnp.int32, (dx, c3), 0) == dx - 1
    for y in range(dy):
        put_pair(pairs_above, y * mx, above[y], last)
    back[...] = back_in[...]

    for sz in range(2):
        for sy in range(2):
            classes, taps = classes_of(sz, sy)
            lhs = jnp.concatenate([act[(pz * 2 + py) * c2 : (pz * 2 + py + 1) * c2, :] for pz, py in classes], axis=0)
            filters = filters_of(kd, taps)
            total = None
            for z in range(dz):
                start, count = z * dy * mx, (dy - sy) * mx
                source, first = (pairs, start) if z + sz < dz else (pairs_above, 0)
                if sz and source is pairs:
                    first = (z + sz) * dy * mx
                cells = source[first + sy * mx : first + dy * mx, :]
                term = dot(lhs[:, start : start + count], cells)
                total = term if total is None else total + term
                if sz:
                    add_grads(back, dot(filters, cells, NT), classes, start, count, c2, True)
            for n, (az, ay) in enumerate(taps):
                deep[az * 3 + ay] = total[n * c2 : (n + 1) * c2]

    for y in range(1, my - 1):
        put_grad(grad.at[y - 1], back, slope[y], y, c2, dy, mx)
    for az in range(3):
        total = None
        for y in range(1, my - 1):
            term = dot(window(even, odd, rim_z, y, az, blk, mx), grad[y - 1], NT)
            total = term if total is None else total + term
        mid[az] = total


def put_grad(dst, back, slope, y, c2, dy, mx):
    for z in range(dst.shape[1] // mx):
        cls = (z % 2) * 2 + y % 2
        at = (z // 2) * dy + y // 2
        value = back[cls * c2 : (cls + 1) * c2, at * mx : (at + 1) * mx] * slope[:, z * mx : (z + 1) * mx]
        dst[:, z * mx : (z + 1) * mx] = value.astype(BF16)


def main_kernel(dims, even, odd, rim_z, act, slope, pairs, pairs_above, back_in, deep_in, mid_in, y_cross, y_pair, km, kd, keep, send, beside, cot_beside, corner, rim_even, rim_odd, rim_pairs, back, grad, sums):
    c1, c2, c3, depth, height, breadth, n_pl, n_gy = dims
    mz, my, mx = depth // 2, height // 2, breadth // 2
    dz, dy, dx = mz // 2, my // 2, mx // 2
    pick = picking_matrix(breadth)
    blk = 3 * c1

    def take(from_below, from_above):
        beside[...] = from_below[...]
        cot_beside[...] = from_above[: (dz + 1) * dx, :c3]

    by_parity("gy", take, y_pair, y_cross)

    for layer in range(depth + 1):
        rim = dot(beside[layer * c1 : (layer + 1) * c1, :], pick)
        if layer == 0:
            dst, at = corner, 0
        else:
            dst, at = (rim_odd, layer // 2) if layer % 2 else (rim_even, layer // 2 - 1)
        place(dst, 0, slice(at * mx, (at + 1) * mx), lambda a: rim[:, a * mx : (a + 1) * mx])
    upper = jnp.concatenate([rim_even[...], even[: 2 * blk, :]], axis=0)
    side = jnp.concatenate([corner[...], rim_z[blk : 3 * blk, :]], axis=0)
    first = [
        jnp.concatenate([side, upper[:, : (mz - 1) * mx]], axis=1),
        jnp.concatenate([rim_odd[...], odd[: 2 * blk, :]], axis=0),
        upper,
    ]

    turned_km = km[...].astype(F32).T.astype(BF16)
    active, low_slope = silu_and_slope(dot(turned_km, jnp.concatenate(first, axis=0)))

    last = lax.broadcasted_iota(jnp.int32, (dx, c3), 0) == dx - 1
    for z in range(dz + 1):
        put_pair(rim_pairs, z * mx, cot_beside[z * dx : (z + 1) * dx, :], last)

    back[...] = back_in[...]
    deep = {(az, ay): deep_in[az * 3 + ay] for az in range(3) for ay in range(3)}
    for sz in range(2):
        for sy in range(2):
            group = [(c, t) for c, t in zip(*classes_of(sz, sy)) if c[1] == sy]
            filters = filters_of(kd, [tap for _, tap in group])
            for z in range(dz):
                lanes = slice((z * dy + dy - 1) * mx, (z * dy + dy) * mx)
                rows = [slice((pz * 2 + py) * c2, (pz * 2 + py + 1) * c2) for (pz, py), _ in group]
                if sy:
                    cells = rim_pairs[(z + sz) * mx : (z + sz + 1) * mx, :]
                    lhs = [act[r, lanes] for r in rows]
                    grads = dot(filters, cells, NT)
                    for n, r in enumerate(rows):
                        back[r, lanes] = back[r, lanes] + grads[n * c2 : (n + 1) * c2]
                else:
                    top = (z + sz) * dy * mx
                    cells = pairs[top : top + mx, :] if z + sz < dz else pairs_above[:mx, :]
                    lhs = [active[:, (2 * z + pz) * mx : (2 * z + pz + 1) * mx] for (pz, py), _ in group]
                term = dot(jnp.concatenate(lhs, axis=0), cells)
                for n, (_, tap) in enumerate(group):
                    deep[tap] = deep[tap] + term[n * c2 : (n + 1) * c2]
    deep = {
        (az * 3 + ay) * 3 + ax: deep[az, ay][:, ax * c3 : (ax + 1) * c3]
        for az in range(3) for ay in range(3) for ax in range(3)
    }

    put_grad(grad.at[0], back, low_slope, 0, c2, dy, mx)
    put_grad(grad.at[1], back, slope[my - 1], my - 1, c2, dy, mx)
    mids = []
    for az in range(3):
        upper_row = dot(window(even, odd, rim_z, my - 1, az, blk, mx), grad[1], NT)
        mids.append(mid_in[az] + dot(first[az], grad[0], NT) + upper_row)
    mid = jnp.concatenate(mids, axis=0)

    share = c3 // n_gy
    per = 448 // (2 * n_pl)
    chunk = (n_gy + 1) * per

    def spread(value, first, offset):
        done = 0
        while done < value.shape[0]:
            k, r = divmod(first + done, per)
            count = min(per - r, value.shape[0] - done)
            core, start = k % 2, k // 2 * chunk + offset + r
            sums[core, start : start + count, :] = value[done : done + count]
            done += count

    for slab in range(14):
        second = deep[2 * slab + 1] if 2 * slab + 1 < 27 else jnp.zeros((c2, c3), F32)
        turned = jnp.concatenate([deep[2 * slab], second], axis=0).T
        for g in range(n_gy):
            spread(turned[g * share : (g + 1) * share], slab * share, g * per)
    half = mid.shape[0] // 2
    packed = jnp.concatenate([mid[:half], mid[half:]], axis=1)
    packed = jnp.concatenate([packed, jnp.zeros((448 - half, 128), F32)], axis=0)
    spread(packed, 0, n_gy * per)
    core = lax.axis_index("core")
    keep[...] = sums[core]
    send[...] = sums[1 - core]


def last_kernel(dims, scales, got, mid_out, deep_out):
    n_all, share, c2, per = dims
    whole = got[...]
    deep = whole[:, :per].reshape(n_all * per, 128) * scales[1]
    mid = whole[:, per:].reshape(n_all * per, 128) * scales[0]
    for a in range(27):
        deep_out[a] = deep[(a // 2) * share : (a // 2 + 1) * share, (a % 2) * c2 : (a % 2 + 1) * c2]
    mid_out[:432] = mid[:432, :64]
    mid_out[432:] = mid[:432, 64:]


def on_device(volume, kernel_mid, kernel_deep, cotangent):
    n_dp = lax.axis_size("dp")
    gz = ("gx", "core")
    n_gz = lax.axis_size(gz)
    n_gy = lax.axis_size("gy")
    samples, c1, depth, height, breadth = volume.shape
    c2, c3 = kernel_mid.shape[0], kernel_deep.shape[0]
    count_mid = n_dp * samples * (n_gz * depth // 2) * (n_gy * height // 2) * (breadth // 2)
    count_deep = n_dp * samples * (n_gz * depth // 4) * (n_gy * height // 4) * (breadth // 4)
    mz, my, mx = depth // 2, height // 2, breadth // 2
    dz, dy, dx = mz // 2, my // 2, mx // 2
    n_pl = n_dp * n_gz // 2
    vol = volume[0]
    cot = cotangent[0].transpose(1, 2, 3, 0)
    in_vmem = pl.BlockSpec(memory_space=pltpu.VMEM)
    layer = vol.reshape(c1, depth * height, breadth)[:, -height:]
    flat = cot.reshape(-1, height, c3)
    cot_layer = jnp.pad(flat, ((0, c1 - flat.shape[0]), (0, 0), (0, breadth - c3)))
    odd = lax.axis_index("core") == 1
    cross, pair = jnp.where(odd, layer, cot_layer), jnp.where(odd, cot_layer, layer)
    z_cross = swapped(cross, gz, 1)
    z_pair = swapped(pair, gz, 0)
    blk = 3 * c1
    own_cells = jax.ShapeDtypeStruct((height * blk, mz * mx), BF16)
    km = kernel_mid.transpose(2, 3, 4, 1, 0).reshape(27 * c1, c2)
    kd = kernel_deep.transpose(2, 3, 4, 1, 0).reshape(27, c2, c3)
    back_shape = jax.ShapeDtypeStruct((4 * c2, dz * dy * mx), F32)
    even, odd = pl.pallas_call(
        functools.partial(gather_kernel, (c1, depth, height, breadth)),
        out_shape=(own_cells, own_cells),
        in_specs=[in_vmem],
        out_specs=(in_vmem, in_vmem),
        scratch_shapes=[
            pltpu.VMEM((2, breadth // 128, c1 * height, 128), F32),
            pltpu.VMEM((2, c1 * height, breadth), BF16),
        ],
        cost_estimate=pl.CostEstimate(flops=2 * c1 * depth * height * breadth * 3 * mx, bytes_accessed=8 << 20, transcendentals=0),
        compiler_params=pltpu.CompilerParams(vmem_limit_bytes=24 * 1024 * 1024),
    )(vol)
    pairs, back = pl.pallas_call(
        back_kernel,
        out_shape=(jax.ShapeDtypeStruct((dz * dy * mx, 3 * c3), BF16), back_shape),
        in_specs=[in_vmem] * 3,
        out_specs=(in_vmem, in_vmem),
        cost_estimate=pl.CostEstimate(flops=2 * 27 * c2 * c3 * dz * dy * dx, bytes_accessed=2 << 20, transcendentals=0),
        compiler_params=pltpu.CompilerParams(vmem_limit_bytes=16 * 1024 * 1024),
    )(cot, kd, odd)
    payload = jax.ShapeDtypeStruct(((depth + 1) * c1, breadth), BF16)
    pair, cross = pl.pallas_call(
        functools.partial(edge_kernel, (c1, depth, height, breadth)),
        out_shape=(payload, payload),
        in_specs=[in_vmem] * 4,
        out_specs=(in_vmem, in_vmem),
        scratch_shapes=[
            pltpu.VMEM((c1, 8, breadth), F32),
            pltpu.VMEM((dx, c3), BF16),
            pltpu.VMEM((4, c1 * 8, 128), F32),
        ],
        compiler_params=pltpu.CompilerParams(vmem_limit_bytes=16 * 1024 * 1024),
    )(vol, cot, z_pair, z_cross)
    pair, cross, even, odd, pairs, back = lax.optimization_barrier((pair, cross, even, odd, pairs, back))
    y_pair, y_cross = swapped(pair, "gy", 0), swapped(cross, "gy", 1)

    share = c3 // n_gy
    per = 448 // (2 * n_pl)
    chunk = (n_gy + 1) * per
    rim_z, act, slope, pairs_above, back, deep, mid = pl.pallas_call(
        functools.partial(early_kernel, (c1, c2, c3, depth, height, breadth)),
        out_shape=(
            jax.ShapeDtypeStruct(((height + 1) * blk, mx), BF16),
            jax.ShapeDtypeStruct((4 * c2, dz * dy * mx), BF16),
            jax.ShapeDtypeStruct((my, c2, mz * mx), F32),
            jax.ShapeDtypeStruct((dy * mx, 3 * c3), BF16),
            back_shape,
            jax.ShapeDtypeStruct((9, c2, 3 * c3), F32),
            jax.ShapeDtypeStruct((3, 3 * blk, c2), F32),
        ),
        in_specs=[in_vmem] * 8,
        out_specs=(in_vmem,) * 7,
        scratch_shapes=[
            pltpu.VMEM((c1 * height, breadth), BF16),
            pltpu.VMEM((dy, dx, c3), BF16),
            pltpu.VMEM((breadth // 128, c1 * height, 128), F32),
            pltpu.VMEM((c1 * height, breadth), BF16),
            pltpu.VMEM((my - 2, c2, mz * mx), BF16),
        ],
        cost_estimate=pl.CostEstimate(flops=2 * c1 * depth * height * breadth * 3 * mx, bytes_accessed=8 << 20, transcendentals=0),
        compiler_params=pltpu.CompilerParams(vmem_limit_bytes=24 * 1024 * 1024),
    )(even, odd, pairs, back, z_pair, z_cross, km, kd)
    keep, send = pl.pallas_call(
        functools.partial(main_kernel, (c1, c2, c3, depth, height, breadth, n_pl, n_gy)),
        out_shape=(jax.ShapeDtypeStruct((n_pl * chunk, 128), F32), jax.ShapeDtypeStruct((n_pl * chunk, 128), F32)),
        in_specs=[in_vmem] * 14,
        out_specs=(in_vmem, in_vmem),
        scratch_shapes=[
            pltpu.VMEM(((depth + 1) * c1, breadth), BF16),
            pltpu.VMEM(((dz + 1) * dx, c3), BF16),
            pltpu.VMEM((blk, mx), BF16),
            pltpu.VMEM((blk, mz * mx), BF16),
            pltpu.VMEM((blk, mz * mx), BF16),
            pltpu.VMEM(((dz + 1) * mx, 3 * c3), BF16),
            pltpu.VMEM((4 * c2, dz * dy * mx), F32),
            pltpu.VMEM((2, c2, mz * mx), BF16),
            pltpu.VMEM((2, n_pl * chunk, 128), F32),
        ],
        compiler_params=pltpu.CompilerParams(vmem_limit_bytes=32 * 1024 * 1024),
    )(even, odd, rim_z, act, slope, pairs, pairs_above, back, deep, mid, y_cross, y_pair, km, kd)
    other = lax.ppermute(send, "core", [(0, 1), (1, 0)])
    pair = (keep + other).astype(BF16).reshape(n_pl, chunk, 128)
    own = jnp.sum(lax.all_to_all(pair, ("dp", "gx"), 0, 0).astype(F32), axis=0)
    deep_own = own[: n_gy * per].reshape(n_gy, per, 128)
    mid_own = jnp.broadcast_to(own[n_gy * per :], (n_gy, per, 128))
    column = jnp.concatenate([deep_own, mid_own], axis=1).astype(BF16)
    own = jnp.sum(lax.all_to_all(column, "gy", 0, 0).astype(F32), axis=0)
    whole = lax.all_gather(own, ("dp", "gx", "core"), axis=0)
    scales = (1.0 / math.sqrt(count_mid), 1.0 / math.sqrt(count_deep))
    mid, deep = pl.pallas_call(
        functools.partial(last_kernel, (2 * n_pl, share, c2, per), scales),
        out_shape=(jax.ShapeDtypeStruct((27 * c1, c2), F32), jax.ShapeDtypeStruct((27, share, c2), F32)),
        in_specs=[in_vmem],
        out_specs=(in_vmem, in_vmem),
        compiler_params=pltpu.CompilerParams(vmem_limit_bytes=24 * 1024 * 1024),
    )(whole)
    mid = mid.reshape(3, 3, 3, c1, c2).transpose(4, 3, 0, 1, 2)
    deep = deep.reshape(3, 3, 3, share, c2).transpose(3, 4, 0, 1, 2)
    return mid, deep


def solution(mesh):
    n_dp, n_gz, n_gy = (mesh.shape[name] for name in ("dp", "gz", "gy"))
    split = Mesh(mesh.devices.reshape(n_dp, n_gz // 2, 2, n_gy), ("dp", "gx", "core", "gy"))
    by_cells = P("dp", None, ("gx", "core"), "gy", None)
    in_specs = (by_cells, P(), P(), by_cells)
    out_specs = (P(), P("gy", None, None, None, None))
    return jax.shard_map(
        on_device, mesh=split, in_specs=in_specs, out_specs=out_specs, check_vma=False
    )
```

```python
import functools
import math

import jax
import jax.numpy as jnp
from jax import lax
from jax.experimental import pallas as pl
from jax.experimental.pallas import tpu as pltpu
from jax.sharding import Mesh, PartitionSpec as P

BF16 = jnp.bfloat16
F32 = jnp.float32
NN = (((1,), (0,)), ((), ()))
NT = (((1,), (1,)), ((), ()))


def dot(a, b, dims=NN):
    return lax.dot_general(a, b, dims, preferred_element_type=F32)


def swapped(block, axis, first):
    count = lax.axis_size(axis)
    route = [(i, i + 1) for i in range(first, count - 1, 2)]
    return lax.ppermute(block, axis, route + [(j, i) for i, j in route])


def picking_matrix(breadth):
    half = breadth // 2
    row = lax.broadcasted_iota(jnp.int32, (breadth, 3 * half), 0)
    col = lax.broadcasted_iota(jnp.int32, (breadth, 3 * half), 1)
    offset = (col >= half).astype(jnp.int32) + (col >= 2 * half).astype(jnp.int32)
    lane = col - offset * half
    odd = (lane >= half // 2).astype(jnp.int32)
    cell = 2 * (lane - odd * (half // 2)) + odd
    return jnp.where(row == 2 * cell + offset - 1, 1.0, 0.0).astype(BF16)


def place(dst, row, lanes, piece):
    c1 = piece(0).shape[0]
    for a in range(3):
        dst[row + a * c1 : row + (a + 1) * c1, lanes] = piece(a).astype(BF16)


def spread_layer(rows, pick, tall, turned, height, put):
    c1 = rows.shape[0] // height
    rows = rows.astype(F32)
    for part in range(tall.shape[0]):
        tall[part, : c1 * height] = rows[:, part * 128 : (part + 1) * 128]
    for y in range(height):
        parts = [tall[part, pl.ds(y, c1, stride=height), :] for part in range(tall.shape[0])]
        turned[y * c1 : (y + 1) * c1, :] = jnp.concatenate(parts, axis=1).astype(BF16)
    cells = dot(turned[...], pick)
    mx = cells.shape[1] // 3
    for y in range(height):
        put(y, lambda a: cells[y * c1 : (y + 1) * c1, a * mx : (a + 1) * mx])


def by_parity(axis, run, pair, cross):
    odd = lax.rem(lax.axis_index(axis), 2)
    pl.when(odd == 1)(lambda: run(pair, cross))
    pl.when(odd == 0)(lambda: run(cross, pair))


def edge_kernel(dims, vol, cot, z_pair, z_cross, pair, cross, below, above, tall):
    c1, depth, height, breadth = dims
    dz, dy, dx, c3 = cot.shape

    def take(from_below, from_above):
        below[...] = from_below[...].astype(F32)[:, height - 8 :]
        above[...] = from_above[: dx // height, :, :c3].reshape(dx, c3)

    by_parity("core", take, z_pair, z_cross)

    def fill(down, up):
        for z in range(depth + 1):
            top = vol[:, z - 1].astype(F32)[:, height - 8 :] if z else below[...]
            top = top.reshape(c1 * 8, breadth)
            for part in range(breadth // 128):
                lanes = slice(part * 128, (part + 1) * 128)
                slot = (z * (breadth // 128) + part) % 4
                tall[slot, : c1 * 8] = top[:, lanes]
                up[z * c1 : (z + 1) * c1, lanes] = tall[slot, pl.ds(7, c1, stride=8), :].astype(BF16)
        for z in range(dz):
            down[z * dx : (z + 1) * dx, :c3] = cot[z, 0]
        down[dz * dx : (dz + 1) * dx, :c3] = above[...]

    by_parity("gy", fill, pair, cross)


def gather_kernel(dims, vol, even, odd, tall, turned):
    c1, depth, height, breadth = dims
    mx = breadth // 2
    pick = picking_matrix(breadth)
    for layer in range(depth):
        rows = vol[:, layer].reshape(c1 * height, breadth)
        dst = even if layer % 2 else odd
        lanes = slice(layer // 2 * mx, (layer // 2 + 1) * mx)
        put = lambda y, piece: place(dst, y * 3 * c1, lanes, piece)
        spread_layer(rows, pick, tall.at[layer % 2], turned.at[layer % 2], height, put)


def back_kernel(cot, kd, order, pairs, back):
    dz, dy, dx, c3 = cot.shape
    c2, mx = kd.shape[1], 2 * dx
    last = lax.broadcasted_iota(jnp.int32, (dx, c3), 0) == dx - 1
    for z in range(dz):
        for y in range(dy):
            put_pair(pairs, (z * dy + y) * mx, cot[z, y], last)
    for sy in range(2):
        classes, taps = classes_of(0, sy)
        filters = filters_of(kd, taps)
        for z in range(dz):
            start, count = z * dy * mx, (dy - sy) * mx
            add_grads(back, dot(filters, pairs[start + sy * mx : start + dy * mx, :], NT), classes, start, count, c2, sy)


def add_grads(back, grads, classes, start, count, c2, held):
    for n, (pz, py) in enumerate(classes):
        rows = slice((pz * 2 + py) * c2, (pz * 2 + py + 1) * c2)
        piece = grads[n * c2 : (n + 1) * c2]
        if held:
            piece = piece + back[rows, start : start + count]
        back[rows, start : start + count] = piece


def silu_and_slope(pre):
    sigma = jax.nn.sigmoid(pre)
    return (pre * sigma).astype(BF16), sigma * (1.0 + pre * (1.0 - sigma))


def put_active(act, active, y, c2, dy, mx):
    for z in range(active.shape[1] // mx):
        cls = (z % 2) * 2 + y % 2
        at = (z // 2) * dy + y // 2
        act[cls * c2 : (cls + 1) * c2, at * mx : (at + 1) * mx] = active[:, z * mx : (z + 1) * mx]


def put_pair(pairs, top, here, last):
    dx = here.shape[0]
    zero = jnp.zeros_like(here)
    moved = jnp.where(last, 0.0, pltpu.roll(here.astype(F32), dx - 1, 0)).astype(BF16)
    pairs[top : top + dx, :] = jnp.concatenate([zero, here, zero], axis=1)
    pairs[top + dx : top + 2 * dx, :] = jnp.concatenate([moved, zero, here], axis=1)


def classes_of(sz, sy):
    classes = [(pz, py) for pz in range(2) for py in range(2) if pz >= sz and py >= sy]
    return classes, [(0 if sz else 1 + pz, 0 if sy else 1 + py) for pz, py in classes]


def filters_of(kd, taps):
    return jnp.concatenate(
        [jnp.concatenate([kd[(az * 3 + ay) * 3 + ax] for ax in range(3)], axis=1) for az, ay in taps], axis=0
    )


def window(even, odd, side, y, az, blk, mx):
    rows = slice((2 * y - 1) * blk, (2 * y + 2) * blk)
    if az == 0:
        return jnp.concatenate([side[2 * y * blk : (2 * y + 3) * blk, :], even[rows, : even.shape[1] - mx]], axis=1)
    return odd[rows, :] if az == 1 else even[rows, :]


def early_kernel(dims, even, odd, pairs, back_in, z_pair, z_cross, km, kd, rim_z, act, slope, pairs_above, back, deep, mid, turned_km, below, above, tall, turned, grad):
    c1, c2, c3, depth, height, breadth = dims
    mz, my, mx = depth // 2, height // 2, breadth // 2
    dz, dy, dx = mz // 2, my // 2, mx // 2
    blk = 3 * c1

    def take(from_below, from_above):
        below[...] = from_below[...].reshape(c1 * height, breadth)
        above[...] = from_above[: dy * dx // height, :, :c3].reshape(dy, dx, c3)

    by_parity("core", take, z_pair, z_cross)
    put = lambda y, piece: place(rim_z, (y + 1) * blk, slice(0, mx), piece)
    spread_layer(below[...], picking_matrix(breadth), tall, turned, height, put)
    turned_km[...] = km[...].astype(F32).T.astype(BF16)
    put_active(act, jnp.zeros((c2, mz * mx), BF16), 0, c2, dy, mx)
    for y in range(1, my):
        cells = jnp.concatenate([window(even, odd, rim_z, y, az, blk, mx) for az in range(3)], axis=0)
        active, slope[y] = silu_and_slope(dot(turned_km[...], cells))
        put_active(act, active, y, c2, dy, mx)

    last = lax.broadcasted_iota(jnp.int32, (dx, c3), 0) == dx - 1
    for y in range(dy):
        put_pair(pairs_above, y * mx, above[y], last)
    back[...] = back_in[...]

    for sz in range(2):
        for sy in range(2):
            classes, taps = classes_of(sz, sy)
            lhs = jnp.concatenate([act[(pz * 2 + py) * c2 : (pz * 2 + py + 1) * c2, :] for pz, py in classes], axis=0)
            filters = filters_of(kd, taps)
            total = None
            for z in range(dz):
                start, count = z * dy * mx, (dy - sy) * mx
                source, first = (pairs, start) if z + sz < dz else (pairs_above, 0)
                if sz and source is pairs:
                    first = (z + sz) * dy * mx
                cells = source[first + sy * mx : first + dy * mx, :]
                term = dot(lhs[:, start : start + count], cells)
                total = term if total is None else total + term
                if sz:
                    add_grads(back, dot(filters, cells, NT), classes, start, count, c2, True)
            for n, (az, ay) in enumerate(taps):
                deep[az * 3 + ay] = total[n * c2 : (n + 1) * c2]

    for y in range(1, my - 1):
        put_grad(grad.at[y - 1], back, slope[y], y, c2, dy, mx)
    for az in range(3):
        total = None
        for y in range(1, my - 1):
            term = dot(window(even, odd, rim_z, y, az, blk, mx), grad[y - 1], NT)
            total = term if total is None else total + term
        mid[az] = total


def put_grad(dst, back, slope, y, c2, dy, mx):
    for z in range(dst.shape[1] // mx):
        cls = (z % 2) * 2 + y % 2
        at = (z // 2) * dy + y // 2
        value = back[cls * c2 : (cls + 1) * c2, at * mx : (at + 1) * mx] * slope[:, z * mx : (z + 1) * mx]
        dst[:, z * mx : (z + 1) * mx] = value.astype(BF16)


def main_kernel(dims, even, odd, rim_z, act, slope, pairs, pairs_above, back_in, deep_in, mid_in, y_cross, y_pair, turned_km, kd, keep, send, beside, cot_beside, corner, rim_even, rim_odd, rim_pairs, top, grad, sums):
    c1, c2, c3, depth, height, breadth, n_pl, n_gy = dims
    mz, my, mx = depth // 2, height // 2, breadth // 2
    dz, dy, dx = mz // 2, my // 2, mx // 2
    pick = picking_matrix(breadth)
    blk = 3 * c1

    def take(from_below, from_above):
        beside[...] = from_below[...]
        cot_beside[...] = from_above[: (dz + 1) * dx, :c3]

    by_parity("gy", take, y_pair, y_cross)

    for layer in range(depth + 1):
        rim = dot(beside[layer * c1 : (layer + 1) * c1, :], pick)
        if layer == 0:
            dst, at = corner, 0
        else:
            dst, at = (rim_odd, layer // 2) if layer % 2 else (rim_even, layer // 2 - 1)
        place(dst, 0, slice(at * mx, (at + 1) * mx), lambda a: rim[:, a * mx : (a + 1) * mx])
    upper = jnp.concatenate([rim_even[...], even[: 2 * blk, :]], axis=0)
    side = jnp.concatenate([corner[...], rim_z[blk : 3 * blk, :]], axis=0)
    first = [
        jnp.concatenate([side, upper[:, : (mz - 1) * mx]], axis=1),
        jnp.concatenate([rim_odd[...], odd[: 2 * blk, :]], axis=0),
        upper,
    ]

    active, low_slope = silu_and_slope(dot(turned_km[...], jnp.concatenate(first, axis=0)))

    last = lax.broadcasted_iota(jnp.int32, (dx, c3), 0) == dx - 1
    for z in range(dz + 1):
        put_pair(rim_pairs, z * mx, cot_beside[z * dx : (z + 1) * dx, :], last)

    deep = {(az, ay): deep_in[az * 3 + ay] for az in range(3) for ay in range(3)}
    for sz in range(2):
        for sy in range(2):
            group = [(c, t) for c, t in zip(*classes_of(sz, sy)) if c[1] == sy]
            filters = filters_of(kd, [tap for _, tap in group])
            for z in range(dz):
                lanes = slice((z * dy + dy - 1) * mx, (z * dy + dy) * mx)
                rows = [slice((pz * 2 + py) * c2, (pz * 2 + py + 1) * c2) for (pz, py), _ in group]
                if sy:
                    cells = rim_pairs[(z + sz) * mx : (z + sz + 1) * mx, :]
                    lhs = [act[r, lanes] for r in rows]
                    grads = dot(filters, cells, NT)
                    for n, ((pz, py), _) in enumerate(group):
                        held = top[2 * z + pz] if sz else back_in[rows[n], lanes]
                        top[2 * z + pz] = held + grads[n * c2 : (n + 1) * c2]
                else:
                    start = (z + sz) * dy * mx
                    cells = pairs[start : start + mx, :] if z + sz < dz else pairs_above[:mx, :]
                    lhs = [active[:, (2 * z + pz) * mx : (2 * z + pz + 1) * mx] for (pz, py), _ in group]
                term = dot(jnp.concatenate(lhs, axis=0), cells)
                for n, (_, tap) in enumerate(group):
                    deep[tap] = deep[tap] + term[n * c2 : (n + 1) * c2]
    deep = {
        (az * 3 + ay) * 3 + ax: deep[az, ay][:, ax * c3 : (ax + 1) * c3]
        for az in range(3) for ay in range(3) for ax in range(3)
    }

    put_grad(grad.at[0], back_in, low_slope, 0, c2, dy, mx)
    for z in range(mz):
        lanes = slice(z * mx, (z + 1) * mx)
        grad[1, :, lanes] = (top[z] * slope[my - 1, :, lanes]).astype(BF16)
    mids = []
    for az in range(3):
        upper_row = dot(window(even, odd, rim_z, my - 1, az, blk, mx), grad[1], NT)
        mids.append(mid_in[az] + dot(first[az], grad[0], NT) + upper_row)
    mid = jnp.concatenate(mids, axis=0)

    share = c3 // n_gy
    per = 448 // (2 * n_pl)
    chunk = (n_gy + 1) * per

    def spread(value, first, offset):
        done = 0
        while done < value.shape[0]:
            k, r = divmod(first + done, per)
            count = min(per - r, value.shape[0] - done)
            core, start = k % 2, k // 2 * chunk + offset + r
            sums[core, start : start + count, :] = value[done : done + count]
            done += count

    for slab in range(14):
        second = deep[2 * slab + 1] if 2 * slab + 1 < 27 else jnp.zeros((c2, c3), F32)
        turned = jnp.concatenate([deep[2 * slab], second], axis=0).T
        for g in range(n_gy):
            spread(turned[g * share : (g + 1) * share], slab * share, g * per)
    half = mid.shape[0] // 2
    packed = jnp.concatenate([mid[:half], mid[half:]], axis=1)
    packed = jnp.concatenate([packed, jnp.zeros((448 - half, 128), F32)], axis=0)
    spread(packed, 0, n_gy * per)
    core = lax.axis_index("core")
    keep[...] = sums[core]
    send[...] = sums[1 - core]


def last_kernel(dims, scales, got, mid_out, deep_out):
    n_all, share, c2, per = dims
    whole = got[...]
    deep = whole[:, :per].reshape(n_all * per, 128) * scales[1]
    mid = whole[:, per:].reshape(n_all * per, 128) * scales[0]
    for a in range(27):
        deep_out[a] = deep[(a // 2) * share : (a // 2 + 1) * share, (a % 2) * c2 : (a % 2 + 1) * c2]
    mid_out[:432] = mid[:432, :64]
    mid_out[432:] = mid[:432, 64:]


def on_device(volume, kernel_mid, kernel_deep, cotangent):
    n_dp = lax.axis_size("dp")
    gz = ("gx", "core")
    n_gz = lax.axis_size(gz)
    n_gy = lax.axis_size("gy")
    samples, c1, depth, height, breadth = volume.shape
    c2, c3 = kernel_mid.shape[0], kernel_deep.shape[0]
    count_mid = n_dp * samples * (n_gz * depth // 2) * (n_gy * height // 2) * (breadth // 2)
    count_deep = n_dp * samples * (n_gz * depth // 4) * (n_gy * height // 4) * (breadth // 4)
    mz, my, mx = depth // 2, height // 2, breadth // 2
    dz, dy, dx = mz // 2, my // 2, mx // 2
    n_pl = n_dp * n_gz // 2
    vol = volume[0]
    cot = cotangent[0].transpose(1, 2, 3, 0)
    in_vmem = pl.BlockSpec(memory_space=pltpu.VMEM)
    layer = vol.reshape(c1, depth * height, breadth)[:, -height:]
    flat = cot.reshape(-1, height, c3)
    cot_layer = jnp.pad(flat, ((0, c1 - flat.shape[0]), (0, 0), (0, breadth - c3)))
    odd = lax.axis_index("core") == 1
    cross, pair = jnp.where(odd, layer, cot_layer), jnp.where(odd, cot_layer, layer)
    z_cross = swapped(cross, gz, 1)
    z_pair = swapped(pair, gz, 0)
    blk = 3 * c1
    own_cells = jax.ShapeDtypeStruct((height * blk, mz * mx), BF16)
    km = kernel_mid.transpose(2, 3, 4, 1, 0).reshape(27 * c1, c2)
    kd = kernel_deep.transpose(2, 3, 4, 1, 0).reshape(27, c2, c3)
    back_shape = jax.ShapeDtypeStruct((4 * c2, dz * dy * mx), F32)
    even, odd = pl.pallas_call(
        functools.partial(gather_kernel, (c1, depth, height, breadth)),
        out_shape=(own_cells, own_cells),
        in_specs=[in_vmem],
        out_specs=(in_vmem, in_vmem),
        scratch_shapes=[
            pltpu.VMEM((2, breadth // 128, (c1 + 1) * height, 128), F32),
            pltpu.VMEM((2, c1 * height, breadth), BF16),
        ],
        cost_estimate=pl.CostEstimate(flops=2 * c1 * depth * height * breadth * 3 * mx, bytes_accessed=8 << 20, transcendentals=0),
        compiler_params=pltpu.CompilerParams(vmem_limit_bytes=24 * 1024 * 1024),
    )(vol)
    pairs, back = pl.pallas_call(
        back_kernel,
        out_shape=(jax.ShapeDtypeStruct((dz * dy * mx, 3 * c3), BF16), back_shape),
        in_specs=[in_vmem] * 3,
        out_specs=(in_vmem, in_vmem),
        cost_estimate=pl.CostEstimate(flops=2 * 27 * c2 * c3 * dz * dy * dx, bytes_accessed=2 << 20, transcendentals=0),
        compiler_params=pltpu.CompilerParams(vmem_limit_bytes=16 * 1024 * 1024),
    )(cot, kd, odd)
    payload = jax.ShapeDtypeStruct(((depth + 1) * c1, breadth), BF16)
    pair, cross = pl.pallas_call(
        functools.partial(edge_kernel, (c1, depth, height, breadth)),
        out_shape=(payload, payload),
        in_specs=[in_vmem] * 4,
        out_specs=(in_vmem, in_vmem),
        scratch_shapes=[
            pltpu.VMEM((c1, 8, breadth), F32),
            pltpu.VMEM((dx, c3), BF16),
            pltpu.VMEM((4, (c1 + 1) * 8, 128), F32),
        ],
        compiler_params=pltpu.CompilerParams(vmem_limit_bytes=16 * 1024 * 1024),
    )(vol, cot, z_pair, z_cross)
    pair, cross, even, odd, pairs, back = lax.optimization_barrier((pair, cross, even, odd, pairs, back))
    y_pair, y_cross = swapped(pair, "gy", 0), swapped(cross, "gy", 1)

    share = c3 // n_gy
    per = 448 // (2 * n_pl)
    chunk = (n_gy + 1) * per
    rim_z, act, slope, pairs_above, back, deep, mid, turned_km = pl.pallas_call(
        functools.partial(early_kernel, (c1, c2, c3, depth, height, breadth)),
        out_shape=(
            jax.ShapeDtypeStruct(((height + 1) * blk, mx), BF16),
            jax.ShapeDtypeStruct((4 * c2, dz * dy * mx), BF16),
            jax.ShapeDtypeStruct((my, c2, mz * mx), F32),
            jax.ShapeDtypeStruct((dy * mx, 3 * c3), BF16),
            back_shape,
            jax.ShapeDtypeStruct((9, c2, 3 * c3), F32),
            jax.ShapeDtypeStruct((3, 3 * blk, c2), F32),
            jax.ShapeDtypeStruct((c2, 27 * c1), BF16),
        ),
        in_specs=[in_vmem] * 8,
        out_specs=(in_vmem,) * 8,
        scratch_shapes=[
            pltpu.VMEM((c1 * height, breadth), BF16),
            pltpu.VMEM((dy, dx, c3), BF16),
            pltpu.VMEM((breadth // 128, (c1 + 1) * height, 128), F32),
            pltpu.VMEM((c1 * height, breadth), BF16),
            pltpu.VMEM((my - 2, c2, mz * mx), BF16),
        ],
        cost_estimate=pl.CostEstimate(flops=2 * c1 * depth * height * breadth * 3 * mx, bytes_accessed=8 << 20, transcendentals=0),
        compiler_params=pltpu.CompilerParams(vmem_limit_bytes=24 * 1024 * 1024),
    )(even, odd, pairs, back, z_pair, z_cross, km, kd)
    keep, send = pl.pallas_call(
        functools.partial(main_kernel, (c1, c2, c3, depth, height, breadth, n_pl, n_gy)),
        out_shape=(jax.ShapeDtypeStruct((n_pl * chunk, 128), F32), jax.ShapeDtypeStruct((n_pl * chunk, 128), F32)),
        in_specs=[in_vmem] * 14,
        out_specs=(in_vmem, in_vmem),
        scratch_shapes=[
            pltpu.VMEM(((depth + 1) * c1, breadth), BF16),
            pltpu.VMEM(((dz + 1) * dx, c3), BF16),
            pltpu.VMEM((blk, mx), BF16),
            pltpu.VMEM((blk, mz * mx), BF16),
            pltpu.VMEM((blk, mz * mx), BF16),
            pltpu.VMEM(((dz + 1) * mx, 3 * c3), BF16),
            pltpu.VMEM((mz, c2, mx), F32),
            pltpu.VMEM((2, c2, mz * mx), BF16),
            pltpu.VMEM((2, n_pl * chunk, 128), F32),
        ],
        compiler_params=pltpu.CompilerParams(vmem_limit_bytes=32 * 1024 * 1024),
    )(even, odd, rim_z, act, slope, pairs, pairs_above, back, deep, mid, y_cross, y_pair, turned_km, kd)
    other = lax.ppermute(send, "core", [(0, 1), (1, 0)])
    pair = (keep + other).astype(BF16).reshape(n_pl, chunk, 128)
    own = jnp.sum(lax.all_to_all(pair, ("dp", "gx"), 0, 0).astype(F32), axis=0)
    deep_own = own[: n_gy * per].reshape(n_gy, per, 128)
    mid_own = jnp.broadcast_to(own[n_gy * per :], (n_gy, per, 128))
    column = jnp.concatenate([deep_own, mid_own], axis=1).astype(BF16)
    own = jnp.sum(lax.all_to_all(column, "gy", 0, 0).astype(F32), axis=0)
    whole = lax.all_gather(own, ("dp", "gx", "core"), axis=0)
    scales = (1.0 / math.sqrt(count_mid), 1.0 / math.sqrt(count_deep))
    mid, deep = pl.pallas_call(
        functools.partial(last_kernel, (2 * n_pl, share, c2, per), scales),
        out_shape=(jax.ShapeDtypeStruct((27 * c1, c2), F32), jax.ShapeDtypeStruct((27, share, c2), F32)),
        in_specs=[in_vmem],
        out_specs=(in_vmem, in_vmem),
        compiler_params=pltpu.CompilerParams(vmem_limit_bytes=24 * 1024 * 1024),
    )(whole)
    mid = mid.reshape(3, 3, 3, c1, c2).transpose(4, 3, 0, 1, 2)
    deep = deep.reshape(3, 3, 3, share, c2).transpose(3, 4, 0, 1, 2)
    return mid, deep


def solution(mesh):
    n_dp, n_gz, n_gy = (mesh.shape[name] for name in ("dp", "gz", "gy"))
    split = Mesh(mesh.devices.reshape(n_dp, n_gz // 2, 2, n_gy), ("dp", "gx", "core", "gy"))
    by_cells = P("dp", None, ("gx", "core"), "gy", None)
    in_specs = (by_cells, P(), P(), by_cells)
    out_specs = (P(), P("gy", None, None, None, None))
    return jax.shard_map(
        on_device, mesh=split, in_specs=in_specs, out_specs=out_specs, check_vma=False
    )
```
